256 devices in a mesh: rep: 32 (over x, z), shard: 8 (over y, core).
Axes of the slice: x: 4, y: 4, z: 8, core: 2. Of those that a mesh axis runs over, the one named last changes fastest.
Arguments:
- grads: bfloat16 [32, 8, 1024, 3968], P('rep', 'shard'), may hold values from -6 to 6
- error: float32 [32, 1024, 3968], P('rep', 'shard'), may hold values from -6 to 6
- q_factor: float32 [32, 3968], replicated, may hold values from -0.09375 to 0.09375
Outputs:
- approx: float32 [1024, 3968], P('shard')
- new_error: float32 [32, 1024, 3968], P('rep', 'shard')
- q_next: float32 [32, 3968], replicated
The draws below stay inside these ranges and needn't reach their ends.
All inputs are finite; a program needn't handle non-finite values.
Results may differ from the reference program's by a relative error of at most 0.0003.
Values sent between devices are 32-bit elements; how exact they have to be, the bound alone decides.
A program may use at most 128 MiB of HBM per device.

```python
import jax
import jax.numpy as jnp
from jax import lax

COLS = 3968
RANK = 32
ROWS = 1024
N_REP = 32
N_SHARD = 8


def with_spikes(values, key, source, target, blocks, factor):
    owner, partner = [(jnp.arange(values.shape[axis_at]) // (values.shape[axis_at] // blocks)).reshape([-1 if axis == axis_at else 1 for axis in range(values.ndim)]) for axis_at in (source, target)]
    chosen = jax.random.permutation(key, blocks)[partner]
    strong = (owner == chosen) | (owner == (partner + blocks // 2) % blocks)
    return jnp.where(strong, factor * values, values)


def levels(rng, dims, shards, smallest, largest):
    loudness, own = 1.0, jax.random.fold_in(rng, 6)
    for position, blocks in shards:
        draws = jnp.exp(jax.random.uniform(jax.random.fold_in(own, position), (blocks,), jnp.float32, smallest / len(shards), largest / len(shards)))
        loudness = loudness * jnp.repeat(draws, dims[position] // blocks).reshape([-1 if axis == position else 1 for axis in range(len(dims))])
    return loudness


def centred(own_key, extent, spread, limit, split=(), dtype=jnp.bfloat16):
    array = spread * jax.random.normal(own_key, extent, jnp.float32)
    if split:
        array = array * levels(own_key, extent, split, -0.22, 0.18)
    return jnp.clip(array, -limit, limit).astype(dtype)


def noise_with(stream_key, shape, scale, bound, pieces, heavy, held_as=jnp.bfloat16):
    array = scale * jax.random.normal(stream_key, shape, jnp.float32)
    if pieces:
        array = array * levels(stream_key, shape, pieces, -0.22, 0.18)
    return jnp.clip(with_spikes(array, jax.random.fold_in(stream_key, 3), *heavy), -bound, bound).astype(held_as)


def setup_inputs(seed: int = 0) -> dict:
    streams_of = jax.random.split(jax.random.key(seed), 4)
    grads = noise_with(streams_of[0], (N_REP, N_SHARD, ROWS, COLS), 1.0, 6.0, ((0, 32), (1, 8)), (1, 2, 8, 2.0))
    error = centred(streams_of[1], (N_REP, ROWS, COLS), 1.0, 6.0, ((0, 32), (1, 8)), jnp.float32)
    q_factor = centred(streams_of[2], (RANK, COLS), COLS ** -0.5, 0.09375, (), jnp.float32)
    return {"grads": grads, "error": error, "q_factor": q_factor}


def merge_rows(grad_terms, error_rows):
    return jnp.sum(grad_terms.astype(jnp.float32), axis=0) + error_rows

def reference(grads, error, q_factor):

    def left_term(pair):
        merged = merge_rows(pair[0], pair[1])
        return jnp.dot(merged.astype(jnp.float32), q_factor.T.astype(jnp.float32), precision=lax.Precision.HIGHEST, preferred_element_type=jnp.float32)
    factor = jnp.sum(lax.map(left_term, (grads, error)), axis=0)
    gram = jnp.dot(factor.T.astype(jnp.float32), factor.astype(jnp.float32), precision=lax.Precision.HIGHEST, preferred_element_type=jnp.float32)
    lower = jnp.linalg.cholesky(gram)
    basis_t = jax.scipy.linalg.solve_triangular(lower, factor.T, lower=True)

    def right_term(pair):
        merged = merge_rows(pair[0], pair[1])
        return jnp.dot(basis_t.astype(jnp.float32), merged.astype(jnp.float32), precision=lax.Precision.HIGHEST, preferred_element_type=jnp.float32)
    q_next = jnp.sum(lax.map(right_term, (grads, error)), axis=0) / N_REP
    approx = jnp.dot(basis_t.T.astype(jnp.float32), q_next.astype(jnp.float32), precision=lax.Precision.HIGHEST, preferred_element_type=jnp.float32)

    def error_term(pair):
        return merge_rows(pair[0], pair[1]) - approx
    new_error = lax.map(error_term, (grads, error))
    return (approx, new_error, q_next)
```

```python
import functools

import jax
import jax.numpy as jnp
from jax import lax
from jax.experimental import pallas as pl
from jax.experimental.pallas import tpu as pltpu
from jax.sharding import PartitionSpec as P

MESH = pl.DeviceIdType.MESH
F32 = jnp.float32
BF16 = jnp.bfloat16
HIGHEST = lax.Precision.HIGHEST
ROWS, COLS, RANK = 1024, 3968, 32
NX, NY, NZ = 4, 4, 8
OWN = 128
HALF = OWN // 2
CHUNK = 16
N_CHUNK = HALF // CHUNK
WIDE = 4096
NT = (((1,), (1,)), ((), ()))
NN = (((1,), (0,)), ((), ()))


def split3(value):
    high = value.astype(BF16)
    rest = value - high.astype(F32)
    middle = rest.astype(BF16)
    low = (rest - middle.astype(F32)).astype(BF16)
    return jnp.concatenate([high, middle, low], axis=0)


def fold3(value):
    return value[:RANK] + value[RANK : 2 * RANK] + value[2 * RANK :]


def inverse_lower(gram):
    row = lax.broadcasted_iota(jnp.int32, (RANK, 2 * RANK), 0)
    col = lax.broadcasted_iota(jnp.int32, (RANK, 2 * RANK), 1)
    work = jnp.concatenate([gram, jnp.zeros((RANK, RANK), F32)], axis=1)
    work = jnp.where(col == row + RANK, 1.0, work)
    scale = jnp.zeros((RANK, 1), F32)
    row1 = lax.broadcasted_iota(jnp.int32, (RANK, 1), 0)
    for j in range(RANK):
        pivot_row = work[j : j + 1, :]
        pivot = work[j : j + 1, j : j + 1]
        factor = jnp.where(row1 > j, work[:, j : j + 1] / pivot, 0.0)
        scale = jnp.where(row1 == j, 1.0 / jnp.sqrt(pivot), scale)
        work = work - factor * pivot_row
    return work[:, RANK:] * scale


def main_kernel(
    g_hbm, e_hbm, q_hbm,
    merged_hbm, usum_hbm, linv_ref, basis_ref,
    g, err, q, qs, psend, precv, far, near, merged, fs, linv,
    bufs_f, bufs_u,
    load_sem, out_sem, p_ss, p_rs, f_ss, f_rs, n_ss, n_rs, ar_f, ar_u,
):
    rep, shard = lax.axis_index("rep"), lax.axis_index("shard")
    x, z = rep // NZ, rep % NZ
    y, c = shard // 2, shard % 2

    def dev(dx, dy, dz, dc):
        return (
            ((x + dx) % NX) * NZ + (z + dz) % NZ,
            ((y + dy) % NY) * 2 + (c + dc) % 2,
        )

    partner = dev(0, 0, 0, 1)
    up, down = dev(0, 1, 0, 0), dev(0, NY - 1, 0, 0)
    x_peers = [dev(j, 0, 0, 0) for j in range(1, NX)]
    z_peers = [dev(0, 0, j, 0) for j in range(1, NZ)]
    y_peers = [dev(2, j, 0, 0) for j in range(1, NY)]
    peers = [partner, up, down, *x_peers, *z_peers, *y_peers]
    sent = []

    def send(src, dst, ss, rs, to):
        copy = pltpu.make_async_remote_copy(
            src_ref=src, dst_ref=dst, send_sem=ss, recv_sem=rs,
            device_id=to, device_id_type=MESH,
        )
        copy.start()
        sent.append(copy)
        return copy

    def first_row(k, t):
        return pl.multiple_of(OWN * (2 * ((y + k) % NY) + (c + t) % 2), OWN)

    def at(k, t):
        return OWN * (2 * k + t)

    q_load = pltpu.make_async_copy(q_hbm, q, load_sem.at[8])
    e_load = pltpu.make_async_copy(e_hbm.at[0], err, load_sem.at[9])
    loads = {}
    for k in (2, 1, 3, 0):
        for t in (1, 0):
            loads[k, t] = pltpu.make_async_copy(
                g_hbm.at[0, 0, pl.ds(first_row(k, t), OWN)],
                g.at[pl.ds(at(k, t), OWN)],
                load_sem.at[2 * k + t],
            )
            loads[k, t].start()
        if k == 2:
            q_load.start()
    e_load.start()

    barrier = pltpu.get_barrier_semaphore()
    for peer in peers:
        pl.semaphore_signal(barrier, 1, device_id=peer, device_id_type=MESH)

    def widen(k, start, rows):
        def step(i, carry):
            at_row = pl.multiple_of(start + i * CHUNK, CHUNK)
            psend[k, pl.ds(at_row, CHUNK), :] = g[
                pl.ds(at(k, 1) + at_row, CHUNK), :
            ].astype(F32)
            return carry

        lax.fori_loop(0, rows // CHUNK, step, 0)

    def to_partner(k, start, rows, i):
        window = (k, pl.ds(start, rows))
        return send(psend.at[window], precv.at[window], p_ss.at[i], p_rs.at[i], partner)

    def add_own(k, start, rows):
        def step(i, carry):
            at_row = pl.multiple_of(start + i * CHUNK, CHUNK)
            precv[k, pl.ds(at_row, CHUNK), :] += g[
                pl.ds(at(k, 0) + at_row, CHUNK), :
            ].astype(F32)
            return carry

        lax.fori_loop(0, rows // CHUNK, step, 0)

    loads[2, 1].wait()
    widen(2, 0, OWN)
    q_load.wait()
    qs[...] = split3(q[...])
    loads[2, 0].wait()
    pl.semaphore_wait(barrier, len(peers))

    order = [(d, i) for i in range(N_CHUNK) for d in (0, 1)]
    copies = {}
    for d, i in order:
        copies[d, i] = to_partner(2, d * HALF + i * CHUNK, CHUNK, d * N_CHUNK + i)
    far_copies = {}
    for d, i in order:
        start = d * HALF + i * CHUNK
        copies[d, i].wait_recv()
        add_own(2, start, CHUNK)
        far_copies[d, i] = send(
            precv.at[2, pl.ds(start, CHUNK)],
            far.at[d, pl.ds(i * CHUNK, CHUNK)],
            f_ss.at[d, i], f_rs.at[d, i], (up, down)[d],
        )

    loads[1, 1].wait()
    loads[1, 0].wait()
    widen(1, HALF, HALF)
    early_up = to_partner(1, HALF, HALF, 8)
    loads[3, 1].wait()
    loads[3, 0].wait()
    widen(3, 0, HALF)
    early_down = to_partner(3, 0, HALF, 9)
    later = {}
    near_copies = {}

    def send_near(d, start, i):
        near_copies[d, i] = send(
            precv.at[(1, 3)[d], pl.ds(start, HALF)],
            near.at[d, pl.ds(start, HALF)],
            n_ss.at[d, i], n_rs.at[d, i], (up, down)[d],
        )

    def near_early():
        early_up.wait_recv()
        add_own(1, HALF, HALF)
        send_near(0, HALF, 0)
        early_down.wait_recv()
        add_own(3, 0, HALF)
        send_near(1, 0, 0)

    def widen_rest():
        widen(1, 0, HALF)
        later[1] = to_partner(1, 0, HALF, 10)
        widen(3, HALF, HALF)
        later[3] = to_partner(3, HALF, HALF, 11)
        widen(0, 0, OWN)
        later[0] = to_partner(0, 0, OWN, 12)

    def near_late():
        for d, k, start in ((0, 1, 0), (1, 3, HALF)):
            later[k].wait_recv()
            for i in range(N_CHUNK):
                far_copies[d, i].wait_recv()

            def step(i, carry, d=d, k=k, start=start):
                at_row = pl.multiple_of(i * CHUNK, CHUNK)
                precv[k, pl.ds(start + at_row, CHUNK), :] = (
                    precv[k, pl.ds(start + at_row, CHUNK), :]
                    + g[pl.ds(at(k, 0) + start + at_row, CHUNK), :].astype(F32)
                    + far[d, pl.ds(at_row, CHUNK), :]
                )
                return carry

            lax.fori_loop(0, N_CHUNK, step, 0)
            send_near(d, start, 1)

    def merge_own():
        later[0].wait_recv()

        def step(i, carry):
            here = pl.ds(pl.multiple_of(i * CHUNK, CHUNK), CHUNK)
            merged[here, :] = (
                precv[0, here, :] + g[here, :].astype(F32) + err[here, :]
            )
            return carry

        lax.fori_loop(0, OWN // CHUNK, step, 0)

    def merge_near(d, i):
        start = ((HALF, 0), (0, HALF))[d][i]
        near_copies[d, i].wait_recv()

        def step(j, carry):
            here = pl.ds(pl.multiple_of(start + j * CHUNK, CHUNK), CHUNK)
            merged[here, :] += near[d, here, :]
            return carry

        lax.fori_loop(0, N_CHUNK, step, 0)

    def all_reduce(width, bufs, sems, beside):
        part, core_in, z_in, x_all, y_all, full = bufs
        ss, rs = sems
        piece = width // NZ
        mine = pl.multiple_of(16 * c, 16)
        theirs = pl.multiple_of(16 * (1 - c), 16)
        at_z = pl.multiple_of(piece * z, 128)

        copy = send(part.at[pl.ds(theirs, 16)], core_in, ss.at[0], rs.at[0], partner)
        beside("core")
        copy.wait_recv()
        core_in[...] += part[pl.ds(mine, 16), :]

        copies = []
        for j, peer in enumerate(z_peers):
            there = pl.multiple_of(piece * ((z + j + 1) % NZ), 128)
            copies.append(
                send(core_in.at[:, pl.ds(there, piece)], z_in.at[j], ss.at[1 + j], rs.at[1 + j], peer)
            )
        beside("z")
        total = core_in[:, pl.ds(at_z, piece)]
        for j, copy in enumerate(copies):
            copy.wait_recv()
            total = total + z_in[j]
        x_all[x] = total

        copies = [
            send(x_all.at[x], x_all.at[x], ss.at[8 + j], rs.at[8 + j], peer)
            for j, peer in enumerate(x_peers)
        ]
        beside("x")
        for copy in copies:
            copy.wait_recv()
        y_all[y] = (x_all[0] + x_all[1]) + (x_all[2] + x_all[3])

        copies = [
            send(y_all.at[y], y_all.at[y], ss.at[11 + j], rs.at[11 + j], peer)
            for j, peer in enumerate(y_peers)
        ]
        beside("y")
        for copy in copies:
            copy.wait_recv()
        window = (pl.ds(mine, 16), pl.ds(at_z, piece))
        full[window] = (y_all[0] + y_all[1]) + (y_all[2] + y_all[3])

        copies = [
            send(full.at[window], full.at[window], ss.at[14 + j], rs.at[14 + j], peer)
            for j, peer in enumerate(z_peers)
        ]
        beside("z2")
        for copy in copies:
            copy.wait_recv()

        window = (pl.ds(mine, 16),)
        copy = send(full.at[window], full.at[window], ss.at[21], rs.at[21], partner)
        beside("core2")
        copy.wait_recv()

    loads[0, 1].wait()
    loads[0, 0].wait()
    e_load.wait()
    part_f = bufs_f[0]
    for k in range(NY):
        terms = fold3(
            lax.dot_general(qs[...], g[pl.ds(at(k, 0), 2 * OWN), :], NT, preferred_element_type=F32)
        )
        for t in (0, 1):
            term = terms[:, OWN * t : OWN * (t + 1)]
            if (k, t) == (0, 0):
                term = term + lax.dot_general(
                    q[...], err[...], NT, precision=HIGHEST, preferred_element_type=F32
                )
            part_f[:, pl.ds(first_row(k, t), OWN)] = term

    def beside_f(phase):
        if phase == "core":
            near_early()
        elif phase == "z":
            widen_rest()
        elif phase == "z2":
            near_late()

    all_reduce(ROWS, bufs_f, ar_f, beside_f)
    factor = bufs_f[5]

    for k in range(NY):
        for t in (0, 1):
            fs[:, pl.ds(at(k, t), OWN)] = split3(factor[:, pl.ds(first_row(k, t), OWN)])
    own_factor = factor[:, pl.ds(first_row(0, 0), OWN)]
    part_u = bufs_u[0]
    for start in range(0, COLS, 1024):
        cols = pl.ds(start, min(1024, COLS - start))
        part_u[:, cols] = fold3(
            lax.dot_general(fs[...], g[:, cols], NN, preferred_element_type=F32)
        ) + lax.dot_general(own_factor, err[:, cols], NN, precision=HIGHEST, preferred_element_type=F32)
    part_u[:, pl.ds(COLS, WIDE - COLS)] = jnp.zeros((RANK, WIDE - COLS), F32)

    def beside_u(phase):
        if phase == "z":
            merge_own()
            whole = factor[...]
            gram = lax.dot_general(whole, whole, NT, precision=HIGHEST, preferred_element_type=F32)
            linv[...] = inverse_lower(gram)
        elif phase == "x":
            linv_ref[...] = linv[...]
            basis_ref[...] = lax.dot_general(
                linv[...], own_factor, NN, precision=HIGHEST, preferred_element_type=F32
            )
        elif phase == "z2":
            merge_near(0, 0)
            merge_near(1, 0)

    all_reduce(WIDE, bufs_u, ar_u, beside_u)
    usum_out = pltpu.make_async_copy(
        bufs_u[5].at[:, pl.ds(0, COLS)], usum_hbm, out_sem.at[0]
    )
    usum_out.start()
    outs = [usum_out]
    for d, start in ((0, 0), (1, HALF)):
        merge_near(d, 1)
        copy = pltpu.make_async_copy(
            merged.at[pl.ds(start, HALF)], merged_hbm.at[pl.ds(start, HALF)], out_sem.at[1 + d]
        )
        copy.start()
        outs.append(copy)
    for copy in sent:
        copy.wait_send()
    for copy in outs:
        copy.wait()


def reduce_buffers(width):
    piece = width // NZ
    return (
        pltpu.VMEM((RANK, width), F32),
        pltpu.VMEM((16, width), F32),
        pltpu.VMEM((NZ - 1, 16, piece), F32),
        pltpu.VMEM((NX, 16, piece), F32),
        pltpu.VMEM((NY, 16, piece), F32),
        pltpu.VMEM((RANK, width), F32),
    )


def final_kernel(n_rep, merged, usum, linv, basis, approx, new_error, q_next):
    @pl.when(pl.program_id(0) == 0)
    def _():
        q_next[...] = lax.dot_general(
            linv[...], usum[...], NN, precision=HIGHEST, preferred_element_type=F32
        ) * (1.0 / n_rep)

    value = lax.dot_general(
        basis[...], q_next[...], NN, precision=HIGHEST, preferred_element_type=F32
    )
    approx[...] = value
    new_error[0] = merged[...] - value


def body(grads, error, q_factor):
    any_space = pl.BlockSpec(memory_space=pl.ANY)
    vmem = pl.BlockSpec(memory_space=pltpu.VMEM)
    dma = pltpu.SemaphoreType.DMA
    merged, usum, linv, basis_t = pl.pallas_call(
        main_kernel,
        out_shape=(
            jax.ShapeDtypeStruct((OWN, COLS), F32),
            jax.ShapeDtypeStruct((RANK, COLS), F32),
            jax.ShapeDtypeStruct((RANK, RANK), F32),
            jax.ShapeDtypeStruct((RANK, OWN), F32),
        ),
        in_specs=[any_space] * 3,
        out_specs=(any_space, any_space, vmem, vmem),
        scratch_shapes=[
            pltpu.VMEM((ROWS, COLS), BF16),
            pltpu.VMEM((OWN, COLS), F32),
            pltpu.VMEM((RANK, COLS), F32),
            pltpu.VMEM((3 * RANK, COLS), BF16),
            pltpu.VMEM((NY, OWN, COLS), F32),
            pltpu.VMEM((NY, OWN, COLS), F32),
            pltpu.VMEM((2, HALF, COLS), F32),
            pltpu.VMEM((2, OWN, COLS), F32),
            pltpu.VMEM((OWN, COLS), F32),
            pltpu.VMEM((3 * RANK, ROWS), BF16),
            pltpu.VMEM((RANK, RANK), F32),
            reduce_buffers(ROWS),
            reduce_buffers(WIDE),
            dma((10,)),
            dma((3,)),
            dma((13,)),
            dma((13,)),
            dma((2, N_CHUNK)),
            dma((2, N_CHUNK)),
            dma((2, 2)),
            dma((2, 2)),
            (dma((22,)), dma((22,))),
            (dma((22,)), dma((22,))),
        ],
        compiler_params=pltpu.CompilerParams(
            collective_id=0, has_side_effects=True, vmem_limit_bytes=56 << 20
        ),
        cost_estimate=pl.CostEstimate(
            flops=1 << 31, bytes_accessed=14 << 20, transcendentals=0
        ),
    )(grads, error, q_factor)
    step = 32
    rows = pl.BlockSpec((step, COLS), lambda i: (i, 0))
    whole = pl.BlockSpec((RANK, COLS), lambda i: (0, 0))
    return pl.pallas_call(
        functools.partial(final_kernel, lax.axis_size("rep")),
        grid=(OWN // step,),
        out_shape=(
            jax.ShapeDtypeStruct((OWN, COLS), F32),
            jax.ShapeDtypeStruct((1, OWN, COLS), F32),
            jax.ShapeDtypeStruct((RANK, COLS), F32),
        ),
        in_specs=[
            rows,
            whole,
            pl.BlockSpec((RANK, RANK), lambda i: (0, 0)),
            pl.BlockSpec((step, RANK), lambda i: (i, 0)),
        ],
        out_specs=(rows, pl.BlockSpec((1, step, COLS), lambda i: (0, i, 0)), whole),
        compiler_params=pltpu.CompilerParams(vmem_limit_bytes=32 << 20),
    )(merged, usum, linv, basis_t.T)


def solution(mesh):
    in_specs = (P("rep", "shard", None, None), P("rep", "shard", None), P())
    out_specs = (P("shard", None), P("rep", "shard", None), P())
    return jax.shard_map(body, mesh=mesh, in_specs=in_specs, out_specs=out_specs, check_vma=False)
```

```python
import functools

import jax
import jax.numpy as jnp
from jax import lax
from jax.experimental import pallas as pl
from jax.experimental.pallas import tpu as pltpu
from jax.sharding import PartitionSpec as P

MESH = pl.DeviceIdType.MESH
F32 = jnp.float32
BF16 = jnp.bfloat16
HIGHEST = lax.Precision.HIGHEST
ROWS, COLS, RANK = 1024, 3968, 32
NX, NY, NZ = 4, 4, 8
OWN = 128
HALF = OWN // 2
CHUNK = 16
N_CHUNK = HALF // CHUNK
N_PART = 4
WIDE = 4096
NT = (((1,), (1,)), ((), ()))
NN = (((1,), (0,)), ((), ()))
TN = (((0,), (0,)), ((), ()))


def split3(value):
    high = value.astype(BF16)
    rest = value - high.astype(F32)
    middle = rest.astype(BF16)
    low = (rest - middle.astype(F32)).astype(BF16)
    return jnp.concatenate([high, middle, low], axis=0)


def fold3(value):
    return value[:RANK] + value[RANK : 2 * RANK] + value[2 * RANK :]


def inverse_lower(gram):
    row = lax.broadcasted_iota(jnp.int32, (RANK, 2 * RANK), 0)
    col = lax.broadcasted_iota(jnp.int32, (RANK, 2 * RANK), 1)
    work = jnp.concatenate([gram, jnp.zeros((RANK, RANK), F32)], axis=1)
    work = jnp.where(col == row + RANK, 1.0, work)
    scale = jnp.zeros((RANK, 1), F32)
    row1 = lax.broadcasted_iota(jnp.int32, (RANK, 1), 0)
    for j in range(RANK):
        pivot_row = work[j : j + 1, :]
        pivot = work[j : j + 1, j : j + 1]
        factor = jnp.where(row1 > j, work[:, j : j + 1] / pivot, 0.0)
        scale = jnp.where(row1 == j, 1.0 / jnp.sqrt(pivot), scale)
        work = work - factor * pivot_row
    return work[:, RANK:] * scale


def main_kernel(
    g_hbm, e_hbm, q_hbm,
    approx, new_error, q_next,
    g, err, q, qs, psend, precv, far, near, fs, linv, basis,
    bufs_f, bufs_u,
    load_sem, p_ss, p_rs, f_ss, f_rs, n_ss, n_rs, ar_f, ar_u, reply,
):
    rep, shard = lax.axis_index("rep"), lax.axis_index("shard")
    x, z = rep // NZ, rep % NZ
    y, c = shard // 2, shard % 2

    def dev(dx, dy, dz, dc):
        return (
            ((x + dx) % NX) * NZ + (z + dz) % NZ,
            ((y + dy) % NY) * 2 + (c + dc) % 2,
        )

    partner = dev(0, 0, 0, 1)
    up, down = dev(0, 1, 0, 0), dev(0, NY - 1, 0, 0)
    x_peers = [dev(j, 0, 0, 0) for j in range(1, NX)]
    z_peers = [dev(0, 0, j, 0) for j in range(1, NZ)]
    y_peers = [dev(2, j, 0, 0) for j in range(1, NY)]
    sent = []
    barrier = pltpu.get_barrier_semaphore()

    def signal(semaphore, peer):
        pl.semaphore_signal(semaphore, 1, device_id=peer, device_id_type=MESH)

    def signal_far(semaphore, above):
        for j, peer in enumerate(z_peers):
            pl.when((z + j + 1 < NZ) == above)(functools.partial(signal, semaphore, peer))
        for j, peer in enumerate(x_peers):
            pl.when((x + j + 1 < NX) == above)(functools.partial(signal, semaphore, peer))
        for peer in y_peers:
            pl.when((x < 2) == above)(functools.partial(signal, semaphore, peer))

    def send(src, dst, ss, rs, to):
        copy = pltpu.make_async_remote_copy(
            src_ref=src, dst_ref=dst, send_sem=ss, recv_sem=rs,
            device_id=to, device_id_type=MESH,
        )
        copy.start()
        sent.append(copy)
        return copy

    def first_row(k, t):
        return pl.multiple_of(OWN * (2 * ((y + k) % NY) + (c + t) % 2), OWN)

    def at(k, t):
        return OWN * (2 * k + t)

    for peer in (partner, up, down):
        signal(barrier, peer)
    q_load = pltpu.make_async_copy(q_hbm, q, load_sem.at[8])
    e_load = pltpu.make_async_copy(e_hbm.at[0], err, load_sem.at[9])
    loads = {}
    for k in (2, 1, 3, 0):
        for t in (1, 0):
            loads[k, t] = pltpu.make_async_copy(
                g_hbm.at[0, 0, pl.ds(first_row(k, t), OWN)],
                g.at[pl.ds(at(k, t), OWN)],
                load_sem.at[2 * k + t],
            )
            loads[k, t].start()
        if k == 2:
            signal_far(barrier, True)
            q_load.start()
    e_load.start()

    def widen(k, start, rows):
        def step(i, carry):
            at_row = pl.multiple_of(start + i * CHUNK, CHUNK)
            psend[k, pl.ds(at_row, CHUNK), :] = g[
                pl.ds(at(k, 1) + at_row, CHUNK), :
            ].astype(F32)
            return carry

        lax.fori_loop(0, rows // CHUNK, step, 0)

    def to_partner(k, start, rows, i):
        window = (k, pl.ds(start, rows))
        return send(psend.at[window], precv.at[window], p_ss.at[i], p_rs.at[i], partner)

    def add_own(k, start, rows):
        def step(i, carry):
            at_row = pl.multiple_of(start + i * CHUNK, CHUNK)
            precv[k, pl.ds(at_row, CHUNK), :] += g[
                pl.ds(at(k, 0) + at_row, CHUNK), :
            ].astype(F32)
            return carry

        lax.fori_loop(0, rows // CHUNK, step, 0)

    loads[2, 1].wait()
    widen(2, 0, OWN)
    pl.semaphore_wait(barrier, 3 + z + x + 3 * (x // 2))

    order = [(d, i) for i in range(N_CHUNK) for d in (0, 1)]
    copies = {}
    for d, i in order:
        copies[d, i] = to_partner(2, d * HALF + i * CHUNK, CHUNK, d * N_CHUNK + i)
    loads[2, 0].wait()
    far_copies = {}
    for d, i in order:
        start = d * HALF + i * CHUNK
        copies[d, i].wait_recv()
        add_own(2, start, CHUNK)
        far_copies[d, i] = send(
            precv.at[2, pl.ds(start, CHUNK)],
            far.at[d, pl.ds(i * CHUNK, CHUNK)],
            f_ss.at[d, i], f_rs.at[d, i], (up, down)[d],
        )

    signal_far(reply, False)

    loads[1, 1].wait()
    loads[1, 0].wait()
    widen(1, HALF, HALF)
    early_up = to_partner(1, HALF, HALF, 8)
    loads[3, 1].wait()
    loads[3, 0].wait()
    widen(3, 0, HALF)
    early_down = to_partner(3, 0, HALF, 9)
    later = {}
    near_copies = {}

    def send_near(d, start, rows, i):
        near_copies[d, i] = send(
            precv.at[(1, 3)[d], pl.ds(start, rows)],
            near.at[d, pl.ds(start, rows)],
            n_ss.at[d, i], n_rs.at[d, i], (up, down)[d],
        )

    def near_early():
        early_up.wait_recv()
        add_own(1, HALF, HALF)
        send_near(0, HALF, HALF, N_CHUNK)
        early_down.wait_recv()
        add_own(3, 0, HALF)
        send_near(1, 0, HALF, N_CHUNK)

    def widen_rest():
        widen(1, 0, HALF)
        later[1] = to_partner(1, 0, HALF, 10)
        widen(3, HALF, HALF)
        later[3] = to_partner(3, HALF, HALF, 11)
        widen(0, 0, OWN)
        later[0] = to_partner(0, 0, OWN, 12)

    def near_late():
        later[1].wait_recv()
        later[3].wait_recv()
        for i in range(N_CHUNK):
            for d, k, start in ((0, 1, 0), (1, 3, HALF)):
                far_copies[d, i].wait_recv()
                here = pl.ds(start + i * CHUNK, CHUNK)
                precv[k, here, :] = (
                    precv[k, here, :]
                    + g[pl.ds(at(k, 0) + start + i * CHUNK, CHUNK), :].astype(F32)
                    + far[d, pl.ds(i * CHUNK, CHUNK), :]
                )
                send_near(d, start + i * CHUNK, CHUNK, i)

    def merge_own():
        later[0].wait_recv()

        def step(i, carry):
            here = pl.ds(pl.multiple_of(i * CHUNK, CHUNK), CHUNK)
            new_error[here, :] = (
                precv[0, here, :] + g[here, :].astype(F32) + err[here, :]
            )
            return carry

        lax.fori_loop(0, OWN // CHUNK, step, 0)

    def merge_early():
        for d, start in ((0, HALF), (1, 0)):
            near_copies[d, N_CHUNK].wait_recv()

            def step(j, carry, d=d, start=start):
                here = pl.ds(pl.multiple_of(start + j * CHUNK, CHUNK), CHUNK)
                new_error[here, :] += near[d, here, :]
                return carry

            lax.fori_loop(0, N_CHUNK, step, 0)

    def all_reduce(width, bufs, sems, beside):
        part, core_in, z_in, x_all, y_all, full = bufs
        ss, rs = sems
        piece = width // NZ
        mine = pl.multiple_of(16 * c, 16)
        theirs = pl.multiple_of(16 * (1 - c), 16)
        at_z = pl.multiple_of(piece * z, 128)

        copy = send(part.at[pl.ds(theirs, 16)], core_in, ss.at[0], rs.at[0], partner)
        beside("core")
        copy.wait_recv()
        core_in[...] += part[pl.ds(mine, 16), :]

        copies = []
        for j, peer in enumerate(z_peers):
            there = pl.multiple_of(piece * ((z + j + 1) % NZ), 128)
            copies.append(
                send(core_in.at[:, pl.ds(there, piece)], z_in.at[j], ss.at[1 + j], rs.at[1 + j], peer)
            )
        beside("z")
        total = core_in[:, pl.ds(at_z, piece)]
        for j, copy in enumerate(copies):
            copy.wait_recv()
            total = total + z_in[j]
        x_all[x] = total

        copies = [
            send(x_all.at[x], x_all.at[x], ss.at[8 + j], rs.at[8 + j], peer)
            for j, peer in enumerate(x_peers)
        ]
        beside("x")
        for copy in copies:
            copy.wait_recv()
        y_all[y] = (x_all[0] + x_all[1]) + (x_all[2] + x_all[3])

        copies = [
            send(y_all.at[y], y_all.at[y], ss.at[11 + j], rs.at[11 + j], peer)
            for j, peer in enumerate(y_peers)
        ]
        beside("y")
        for copy in copies:
            copy.wait_recv()
        window = (pl.ds(mine, 16), pl.ds(at_z, piece))
        full[window] = (y_all[0] + y_all[1]) + (y_all[2] + y_all[3])

        copies = [
            send(full.at[window], full.at[window], ss.at[14 + j], rs.at[14 + j], peer)
            for j, peer in enumerate(z_peers)
        ]
        beside("z2")
        for copy in copies:
            copy.wait_recv()

        window = (pl.ds(mine, 16),)
        copy = send(full.at[window], full.at[window], ss.at[21], rs.at[21], partner)
        beside("core2")
        copy.wait_recv()

    loads[0, 1].wait()
    loads[0, 0].wait()
    e_load.wait()
    q_load.wait()
    qs[...] = split3(q[...])
    part_f = bufs_f[0]
    for k in range(NY):
        terms = fold3(
            lax.dot_general(qs[...], g[pl.ds(at(k, 0), 2 * OWN), :], NT, preferred_element_type=F32)
        )
        for t in (0, 1):
            term = terms[:, OWN * t : OWN * (t + 1)]
            if (k, t) == (0, 0):
                term = term + lax.dot_general(
                    q[...], err[...], NT, precision=HIGHEST, preferred_element_type=F32
                )
            part_f[:, pl.ds(first_row(k, t), OWN)] = term

    def beside_f(phase):
        if phase == "core":
            near_early()
            answers = (NZ - 1 - z) + (NX - 1 - x) + 3 * (1 - x // 2)

            @pl.when(answers > 0)
            def _():
                pl.semaphore_wait(reply, answers)
        elif phase == "z":
            widen_rest()
        elif phase == "z2":
            near_late()

    all_reduce(ROWS, bufs_f, ar_f, beside_f)
    factor = bufs_f[5]

    for k in range(NY):
        for t in (0, 1):
            fs[:, pl.ds(at(k, t), OWN)] = split3(factor[:, pl.ds(first_row(k, t), OWN)])
    own_factor = factor[:, pl.ds(first_row(0, 0), OWN)]
    part_u = bufs_u[0]
    for start in range(0, COLS, 1024):
        cols = pl.ds(start, min(1024, COLS - start))
        part_u[:, cols] = fold3(
            lax.dot_general(fs[...], g[:, cols], NN, preferred_element_type=F32)
        ) + lax.dot_general(own_factor, err[:, cols], NN, precision=HIGHEST, preferred_element_type=F32)
    part_u[:, pl.ds(COLS, WIDE - COLS)] = jnp.zeros((RANK, WIDE - COLS), F32)

    def beside_u(phase):
        if phase == "z":
            merge_own()
            whole = factor[...]
            gram = lax.dot_general(whole, whole, NT, precision=HIGHEST, preferred_element_type=F32)
            linv[...] = inverse_lower(gram)
        elif phase == "x":
            basis[...] = lax.dot_general(
                linv[...], own_factor, NN, precision=HIGHEST, preferred_element_type=F32
            )
        elif phase == "z2":
            merge_early()

    all_reduce(WIDE, bufs_u, ar_u, beside_u)
    for start in range(0, COLS, 1024):
        cols = pl.ds(start, min(1024, COLS - start))
        right = lax.dot_general(
            linv[...], bufs_u[5][:, cols], NN, precision=HIGHEST, preferred_element_type=F32
        ) * (1.0 / (NX * NZ))
        q_next[:, cols] = right
        value = lax.dot_general(
            basis[...], right, TN, precision=HIGHEST, preferred_element_type=F32
        )
        approx[:, cols] = value
        new_error[:, cols] -= value
    for i in range(N_CHUNK):
        for d, start in ((0, 0), (1, HALF)):
            near_copies[d, i].wait_recv()
            here = pl.ds(start + i * CHUNK, CHUNK)
            new_error[here, :] += near[d, here, :]
    for copy in sent:
        copy.wait_send()


def reduce_buffers(width):
    piece = width // NZ
    return (
        pltpu.VMEM((RANK, width), F32),
        pltpu.VMEM((16, width), F32),
        pltpu.VMEM((NZ - 1, 16, piece), F32),
        pltpu.VMEM((NX, 16, piece), F32),
        pltpu.VMEM((NY, 16, piece), F32),
        pltpu.VMEM((RANK, width), F32),
    )


def out_kernel(approx, new_error, q_next, approx_out, new_error_out, q_out, sem):
    copies = [pltpu.make_async_copy(q_next, q_out, sem.at[0])]
    for i in range(N_PART):
        rows = pl.ds(i * (OWN // N_PART), OWN // N_PART)
        copies.append(
            pltpu.make_async_copy(approx.at[rows], approx_out.at[rows], sem.at[1 + 2 * i])
        )
        copies.append(
            pltpu.make_async_copy(
                new_error.at[rows], new_error_out.at[0, rows], sem.at[2 + 2 * i]
            )
        )
    for copy in copies:
        copy.start()
    for copy in copies:
        copy.wait()


def body(grads, error, q_factor):
    any_space = pl.BlockSpec(memory_space=pl.ANY)
    vmem = pl.BlockSpec(memory_space=pltpu.VMEM)
    dma = pltpu.SemaphoreType.DMA
    results = pl.pallas_call(
        main_kernel,
        out_shape=(
            pltpu.VMEM((OWN, COLS), F32),
            pltpu.VMEM((OWN, COLS), F32),
            pltpu.VMEM((RANK, COLS), F32),
        ),
        in_specs=[any_space] * 3,
        out_specs=(vmem,) * 3,
        scratch_shapes=[
            pltpu.VMEM((ROWS, COLS), BF16),
            pltpu.VMEM((OWN, COLS), F32),
            pltpu.VMEM((RANK, COLS), F32),
            pltpu.VMEM((3 * RANK, COLS), BF16),
            pltpu.VMEM((NY, OWN, COLS), F32),
            pltpu.VMEM((NY, OWN, COLS), F32),
            pltpu.VMEM((2, HALF, COLS), F32),
            pltpu.VMEM((2, OWN, COLS), F32),
            pltpu.VMEM((3 * RANK, ROWS), BF16),
            pltpu.VMEM((RANK, RANK), F32),
            pltpu.VMEM((RANK, OWN), F32),
            reduce_buffers(ROWS),
            reduce_buffers(WIDE),
            dma((10,)),
            dma((13,)),
            dma((13,)),
            dma((2, N_CHUNK)),
            dma((2, N_CHUNK)),
            dma((2, N_CHUNK + 1)),
            dma((2, N_CHUNK + 1)),
            (dma((22,)), dma((22,))),
            (dma((22,)), dma((22,))),
            pltpu.SemaphoreType.REGULAR,
        ],
        compiler_params=pltpu.CompilerParams(
            collective_id=0, has_side_effects=True, vmem_limit_bytes=48 << 20
        ),
        cost_estimate=pl.CostEstimate(
            flops=1 << 31, bytes_accessed=14 << 20, transcendentals=0
        ),
    )(grads, error, pltpu.with_memory_space_constraint(q_factor, pltpu.HBM))
    return pl.pallas_call(
        out_kernel,
        out_shape=(
            jax.ShapeDtypeStruct((OWN, COLS), F32),
            jax.ShapeDtypeStruct((1, OWN, COLS), F32),
            jax.ShapeDtypeStruct((RANK, COLS), F32),
        ),
        in_specs=[vmem] * 3,
        out_specs=(any_space,) * 3,
        scratch_shapes=[dma((1 + 2 * N_PART,))],
        compiler_params=pltpu.CompilerParams(vmem_limit_bytes=16 << 20),
    )(*results)


def solution(mesh):
    in_specs = (P("rep", "shard", None, None), P("rep", "shard", None), P())
    out_specs = (P("shard", None), P("rep", "shard", None), P())
    return jax.shard_map(body, mesh=mesh, in_specs=in_specs, out_specs=out_specs, check_vma=False)
```

```python
import functools

import jax
import jax.numpy as jnp
from jax import lax
from jax.experimental import pallas as pl
from jax.experimental.pallas import tpu as pltpu
from jax.sharding import PartitionSpec as P

MESH = pl.DeviceIdType.MESH
F32 = jnp.float32
BF16 = jnp.bfloat16
HIGHEST = lax.Precision.HIGHEST
ROWS, COLS, RANK = 1024, 3968, 32
NX, NY, NZ = 4, 4, 8
OWN = 128
HALF = OWN // 2
CHUNK = 16
N_CHUNK = HALF // CHUNK
N_PART = 4
WIDE = 4096
NT = (((1,), (1,)), ((), ()))
NN = (((1,), (0,)), ((), ()))


def split(value):
    high = value.astype(BF16)
    rest = value - high.astype(F32)
    middle = rest.astype(BF16)
    low = (rest - middle.astype(F32)).astype(BF16)
    return high, middle, low


def split3(value):
    return jnp.concatenate(split(value), axis=0)


def left6(value):
    high, middle, low = (term.astype(F32) for term in split(value))
    return jnp.concatenate([high, high, middle, high, low, middle], axis=0).T.astype(BF16)


def right6(value):
    high, middle, low = split(value)
    return jnp.concatenate([high, middle, high, low, high, middle], axis=0)


def fold3(value):
    return value[:RANK] + value[RANK : 2 * RANK] + value[2 * RANK : 3 * RANK]


def inverse_lower(gram):
    row = lax.broadcasted_iota(jnp.int32, (RANK, 2 * RANK), 0)
    col = lax.broadcasted_iota(jnp.int32, (RANK, 2 * RANK), 1)
    work = jnp.concatenate([gram, jnp.zeros((RANK, RANK), F32)], axis=1)
    work = jnp.where(col == row + RANK, 1.0, work)
    scale = jnp.zeros((RANK, 1), F32)
    row1 = lax.broadcasted_iota(jnp.int32, (RANK, 1), 0)
    for j in range(RANK):
        pivot_row = work[j : j + 1, :]
        pivot = work[j : j + 1, j : j + 1]
        factor = jnp.where(row1 > j, work[:, j : j + 1] / pivot, 0.0)
        scale = jnp.where(row1 == j, 1.0 / jnp.sqrt(pivot), scale)
        work = work - factor * pivot_row
    return work[:, RANK:] * scale


def main_kernel(
    g_hbm, e_hbm, q_hbm,
    approx, new_error, q_next,
    g, err, q, qs, psend, precv, far, near, fs, linv6, basis6,
    bufs_f, bufs_u,
    load_sem, far_sem, p_ss, p_rs, f_ss, f_rs, n_ss, n_rs, ar_f, ar_u, reply, ring,
):
    rep, shard = lax.axis_index("rep"), lax.axis_index("shard")
    x, z = rep // NZ, rep % NZ
    y, c = shard // 2, shard % 2

    def dev(dx, dy, dz, dc):
        return (
            ((x + dx) % NX) * NZ + (z + dz) % NZ,
            ((y + dy) % NY) * 2 + (c + dc) % 2,
        )

    partner = dev(0, 0, 0, 1)
    up, down = dev(0, 1, 0, 0), dev(0, NY - 1, 0, 0)
    x_peers = [dev(j, 0, 0, 0) for j in range(1, NX)]
    z_peers = [dev(0, 0, j, 0) for j in range(1, NZ)]
    y_peers = [dev(2, j, 0, 0) for j in range(1, NY)]
    sent = []
    barrier = pltpu.get_barrier_semaphore()

    def signal(semaphore, peer):
        pl.semaphore_signal(semaphore, 1, device_id=peer, device_id_type=MESH)

    def place(at_x):
        return at_x + (at_x == 2) - (at_x == 3)

    def signal_far(semaphore, above):
        for j, peer in enumerate(z_peers):
            pl.when((z + j + 1 < NZ) == above)(functools.partial(signal, semaphore, peer))
        for j, peer in enumerate(x_peers):
            pl.when((place((x + j + 1) % NX) > place(x)) == above)(functools.partial(signal, semaphore, peer))

    def send(src, dst, ss, rs, to):
        copy = pltpu.make_async_remote_copy(
            src_ref=src, dst_ref=dst, send_sem=ss, recv_sem=rs,
            device_id=to, device_id_type=MESH,
        )
        copy.start()
        sent.append(copy)
        return copy

    def first_row(k, t):
        return pl.multiple_of(OWN * (2 * ((y + k) % NY) + (c + t) % 2), OWN)

    def at(k, t):
        return OWN * (2 * k + t)

    for peer in (partner, up, down):
        signal(barrier, peer)
    q_load = pltpu.make_async_copy(q_hbm, q, load_sem.at[8])
    e_load = pltpu.make_async_copy(e_hbm.at[0], err, load_sem.at[9])
    loads = {
        (k, t): pltpu.make_async_copy(
            g_hbm.at[0, 0, pl.ds(first_row(k, t), OWN)],
            g.at[pl.ds(at(k, t), OWN)],
            load_sem.at[2 * k + t],
        )
        for k in (1, 3, 0)
        for t in (1, 0)
    }
    pieces = {0: (0, CHUNK), 1: (CHUNK, HALF - CHUNK)}
    far_loads = {
        (i, t, d): pltpu.make_async_copy(
            g_hbm.at[0, 0, pl.ds(first_row(2, t) + d * HALF + start, rows)],
            g.at[pl.ds(at(2, t) + d * HALF + start, rows)],
            far_sem.at[i, t, d],
        )
        for i, (start, rows) in pieces.items()
        for t in (1, 0)
        for d in (0, 1)
    }
    for load in far_loads.values():
        load.start()
    signal_far(barrier, True)

    def widen(k, start, rows):
        def step(i, carry):
            at_row = pl.multiple_of(start + i * CHUNK, CHUNK)
            psend[k, pl.ds(at_row, CHUNK), :] = g[
                pl.ds(at(k, 1) + at_row, CHUNK), :
            ].astype(F32)
            return carry

        lax.fori_loop(0, rows // CHUNK, step, 0)

    def to_partner(k, start, rows, i):
        window = (k, pl.ds(start, rows))
        return send(psend.at[window], precv.at[window], p_ss.at[i], p_rs.at[i], partner)

    def add_own(k, start, rows):
        def step(i, carry):
            at_row = pl.multiple_of(start + i * CHUNK, CHUNK)
            precv[k, pl.ds(at_row, CHUNK), :] += g[
                pl.ds(at(k, 0) + at_row, CHUNK), :
            ].astype(F32)
            return carry

        lax.fori_loop(0, rows // CHUNK, step, 0)

    for d in (0, 1):
        far_loads[0, 1, d].wait()
        widen(2, d * HALF, CHUNK)
    q_load.start()
    e_load.start()
    for load in loads.values():
        load.start()
    pl.semaphore_wait(barrier, 3 + z + place(x))

    order = [(d, i) for i in range(N_CHUNK) for d in (0, 1)]
    copies = {}
    far_copies = {}
    for d, i in order:
        if (d, i) == (0, 1):
            for e in (0, 1):
                far_loads[1, 1, e].wait()
                widen(2, e * HALF + CHUNK, HALF - CHUNK)
        copies[d, i] = to_partner(2, d * HALF + i * CHUNK, CHUNK, d * N_CHUNK + i)
    for d, i in order:
        if i < 2:
            far_loads[i, 0, d].wait()
        start = d * HALF + i * CHUNK
        copies[d, i].wait_recv()
        add_own(2, start, CHUNK)
        far_copies[d, i] = send(
            precv.at[2, pl.ds(start, CHUNK)],
            far.at[d, pl.ds(i * CHUNK, CHUNK)],
            f_ss.at[d, i], f_rs.at[d, i], (up, down)[d],
        )
    signal_far(reply, False)
    for peer in (up, down):
        signal(ring, peer)

    q_load.wait()
    qs[pl.ds(0, 3 * RANK), :] = split3(q[...])
    qs[pl.ds(3 * RANK, RANK), :] = jnp.zeros((RANK, COLS), BF16)
    e_load.wait()

    def split_error(i, carry):
        at_row = pl.multiple_of(i * CHUNK, CHUNK)
        for j, term in enumerate(split(err[pl.ds(at_row, CHUNK), :])):
            g[pl.ds(ROWS + j * OWN + at_row, CHUNK), :] = term
        return carry

    lax.fori_loop(0, OWN // CHUNK, split_error, 0)
    for load in loads.values():
        load.wait()
    early = {}
    later = {}
    near_copies = {}

    def send_near(d, start, rows, i):
        near_copies[d, i] = send(
            precv.at[(1, 3)[d], pl.ds(start, rows)],
            near.at[d, pl.ds(start, rows)],
            n_ss.at[d, i], n_rs.at[d, i], (up, down)[d],
        )

    def widen_early():
        widen(1, HALF, HALF)
        early[1] = to_partner(1, HALF, HALF, 8)
        widen(3, 0, HALF)
        early[3] = to_partner(3, 0, HALF, 9)

    def near_early():
        early[1].wait_recv()
        add_own(1, HALF, HALF)
        send_near(0, HALF, HALF, N_CHUNK)
        early[3].wait_recv()
        add_own(3, 0, HALF)
        send_near(1, 0, HALF, N_CHUNK)

    def widen_rest():
        widen(1, 0, HALF)
        later[1] = to_partner(1, 0, HALF, 10)
        widen(3, HALF, HALF)
        later[3] = to_partner(3, HALF, HALF, 11)
        widen(0, 0, OWN)
        later[0] = to_partner(0, 0, OWN, 12)

    def near_late():
        later[1].wait_recv()
        later[3].wait_recv()
        for i in range(N_CHUNK):
            for d, k, start in ((0, 1, 0), (1, 3, HALF)):
                far_copies[d, i].wait_recv()
                here = pl.ds(start + i * CHUNK, CHUNK)
                precv[k, here, :] = (
                    precv[k, here, :]
                    + g[pl.ds(at(k, 0) + start + i * CHUNK, CHUNK), :].astype(F32)
                    + far[d, pl.ds(i * CHUNK, CHUNK), :]
                )
                send_near(d, start + i * CHUNK, CHUNK, i)

    def merge_own():
        later[0].wait_recv()

        def step(i, carry):
            here = pl.ds(pl.multiple_of(i * CHUNK, CHUNK), CHUNK)
            new_error[here, :] = (
                precv[0, here, :] + g[here, :].astype(F32) + err[here, :]
            )
            return carry

        lax.fori_loop(0, OWN // CHUNK, step, 0)

    def merge_early():
        for d, start in ((0, HALF), (1, 0)):
            near_copies[d, N_CHUNK].wait_recv()

            def step(j, carry, d=d, start=start):
                here = pl.ds(pl.multiple_of(start + j * CHUNK, CHUNK), CHUNK)
                new_error[here, :] += near[d, here, :]
                return carry

            lax.fori_loop(0, N_CHUNK, step, 0)

    def all_reduce(width, bufs, sems, beside):
        part, core_in, z_in, x_all, x_sum, y_all, full = bufs
        ss, rs = sems
        piece = width // NZ
        mine = pl.multiple_of(16 * c, 16)
        theirs = pl.multiple_of(16 * (1 - c), 16)
        at_z = pl.multiple_of(piece * z, 128)

        copy = send(part.at[pl.ds(theirs, 16)], core_in, ss.at[0], rs.at[0], partner)
        beside("core")
        copy.wait_recv()
        core_in[...] += part[pl.ds(mine, 16), :]

        copies = []
        for j, peer in enumerate(z_peers):
            there = pl.multiple_of(piece * ((z + j + 1) % NZ), 128)
            copies.append(
                send(core_in.at[:, pl.ds(there, piece)], z_in.at[j], ss.at[1 + j], rs.at[1 + j], peer)
            )
        beside("z")
        total = core_in[:, pl.ds(at_z, piece)]
        for j, copy in enumerate(copies):
            copy.wait_recv()
            total = total + z_in[j]
        x_all[x] = total

        copies = [
            send(x_all.at[x], x_all.at[x], ss.at[8 + j], rs.at[8 + j], peer)
            for j, peer in enumerate(x_peers)
        ]
        beside("x")
        for copy in copies:
            copy.wait_recv()
        total = (x_all[0] + x_all[1]) + (x_all[2] + x_all[3])
        quartered = y_all.shape[-1] < piece
        if quartered:
            quarter = piece // NX
            x_sum[...] = total
            y_all[y] = x_sum[:, pl.ds(pl.multiple_of(quarter * x, 128), quarter)]
            source = x_sum.at[:, pl.ds(pl.multiple_of(quarter * ((x + 2) % NX), 128), quarter)]
            window = (pl.ds(mine, 16), pl.ds(pl.multiple_of(at_z + quarter * x, 128), quarter))
        else:
            y_all[y] = total
            source = y_all.at[y]
            window = (pl.ds(mine, 16), pl.ds(at_z, piece))

        copies = [
            send(source, y_all.at[y], ss.at[11 + j], rs.at[11 + j], peer)
            for j, peer in enumerate(y_peers)
        ]
        beside("y")
        for copy in copies:
            copy.wait_recv()
        full[window] = (y_all[0] + y_all[1]) + (y_all[2] + y_all[3])
        if quartered:
            copies = [
                send(full.at[window], full.at[window], ss.at[22 + j], rs.at[22 + j], peer)
                for j, peer in enumerate(x_peers)
            ]
            for copy in copies:
                copy.wait_recv()
            window = (pl.ds(mine, 16), pl.ds(at_z, piece))

        copies = [
            send(full.at[window], full.at[window], ss.at[14 + j], rs.at[14 + j], peer)
            for j, peer in enumerate(z_peers)
        ]
        beside("z2")
        for copy in copies:
            copy.wait_recv()

        window = (pl.ds(mine, 16),)
        copy = send(full.at[window], full.at[window], ss.at[21], rs.at[21], partner)
        beside("core2")
        copy.wait_recv()

    part_f = bufs_f[0]

    def left_terms(start, rows):
        terms = lax.dot_general(
            g[pl.ds(start, rows), :], qs[...], NT, preferred_element_type=F32
        )
        return fold3(terms.T)

    for k in (1, 2, 3):
        terms = left_terms(at(k, 0), 2 * OWN)
        for t in (0, 1):
            part_f[:, pl.ds(first_row(k, t), OWN)] = terms[:, OWN * t : OWN * (t + 1)]
    terms = left_terms(0, 2 * OWN)
    own = left_terms(ROWS, 3 * OWN)
    part_f[:, pl.ds(first_row(0, 1), OWN)] = terms[:, OWN:]
    part_f[:, pl.ds(first_row(0, 0), OWN)] = (
        terms[:, :OWN] + own[:, :OWN] + own[:, OWN : 2 * OWN] + own[:, 2 * OWN :]
    )

    def beside_f(phase):
        if phase == "core":
            pl.semaphore_wait(ring, 2)
            answers = (NZ - 1 - z) + (NX - 1 - place(x))

            @pl.when(answers > 0)
            def _():
                pl.semaphore_wait(reply, answers)

        elif phase == "z":
            widen_early()
        elif phase == "x":
            near_early()
        elif phase == "y":
            widen_rest()
        elif phase == "z2":
            near_late()

    all_reduce(ROWS, bufs_f, ar_f, beside_f)
    factor = bufs_f[6]

    for k in range(NY):
        for t in (0, 1):
            fs[:, pl.ds(at(k, t), OWN)] = split3(factor[:, pl.ds(first_row(k, t), OWN)])
    own_factor = factor[:, pl.ds(first_row(0, 0), OWN)]
    for j in range(3):
        fs[:, pl.ds(ROWS + j * OWN, OWN)] = split3(own_factor)
    part_u = bufs_u[0]
    for start in range(0, COLS, 1024):
        cols = pl.ds(start, min(1024, COLS - start))
        part_u[:, cols] = fold3(
            lax.dot_general(fs[...], g[:, cols], NN, preferred_element_type=F32)
        )
    part_u[:, pl.ds(COLS, WIDE - COLS)] = jnp.zeros((RANK, WIDE - COLS), F32)

    def beside_u(phase):
        if phase == "z":
            merge_own()
            whole = factor[...]
            gram = lax.dot_general(whole, whole, NT, precision=HIGHEST, preferred_element_type=F32)
            linv = inverse_lower(gram)
            linv6[...] = left6((linv * (1.0 / (NX * NZ))).T)
            basis = lax.dot_general(
                linv, own_factor, NN, precision=HIGHEST, preferred_element_type=F32
            )
            basis6[...] = left6(basis)
        elif phase == "z2":
            merge_early()

    all_reduce(WIDE, bufs_u, ar_u, beside_u)
    for start in range(0, COLS, 1024):
        cols = pl.ds(start, min(1024, COLS - start))
        right = lax.dot_general(
            linv6[...], right6(bufs_u[6][:, cols]), NN, preferred_element_type=F32
        )
        q_next[:, cols] = right
        value = lax.dot_general(basis6[...], right6(right), NN, preferred_element_type=F32)
        approx[:, cols] = value
        new_error[:, cols] -= value
    for i in range(N_CHUNK):
        for d, start in ((0, 0), (1, HALF)):
            near_copies[d, i].wait_recv()
            here = pl.ds(start + i * CHUNK, CHUNK)
            new_error[here, :] += near[d, here, :]
    for copy in sent:
        copy.wait_send()


def reduce_buffers(width, quartered):
    piece = width // NZ
    return (
        pltpu.VMEM((RANK, width), F32),
        pltpu.VMEM((16, width), F32),
        pltpu.VMEM((NZ - 1, 16, piece), F32),
        pltpu.VMEM((NX, 16, piece), F32),
        pltpu.VMEM((16, piece), F32),
        pltpu.VMEM((NY, 16, piece // NX if quartered else piece), F32),
        pltpu.VMEM((RANK, width), F32),
    )


def out_kernel(approx, new_error, q_next, approx_out, new_error_out, q_out, sem):
    copies = [pltpu.make_async_copy(q_next, q_out, sem.at[0])]
    for i in range(N_PART):
        rows = pl.ds(i * (OWN // N_PART), OWN // N_PART)
        copies.append(
            pltpu.make_async_copy(approx.at[rows], approx_out.at[rows], sem.at[1 + 2 * i])
        )
        copies.append(
            pltpu.make_async_copy(
                new_error.at[rows], new_error_out.at[0, rows], sem.at[2 + 2 * i]
            )
        )
    for copy in copies:
        copy.start()
    for copy in copies:
        copy.wait()


def body(grads, error, q_factor):
    any_space = pl.BlockSpec(memory_space=pl.ANY)
    vmem = pl.BlockSpec(memory_space=pltpu.VMEM)
    dma = pltpu.SemaphoreType.DMA
    results = pl.pallas_call(
        main_kernel,
        out_shape=(
            pltpu.VMEM((OWN, COLS), F32),
            pltpu.VMEM((OWN, COLS), F32),
            pltpu.VMEM((RANK, COLS), F32),
        ),
        in_specs=[any_space] * 3,
        out_specs=(vmem,) * 3,
        scratch_shapes=[
            pltpu.VMEM((ROWS + 3 * OWN, COLS), BF16),
            pltpu.VMEM((OWN, COLS), F32),
            pltpu.VMEM((RANK, COLS), F32),
            pltpu.VMEM((4 * RANK, COLS), BF16),
            pltpu.VMEM((NY, OWN, COLS), F32),
            pltpu.VMEM((NY, OWN, COLS), F32),
            pltpu.VMEM((2, HALF, COLS), F32),
            pltpu.VMEM((2, OWN, COLS), F32),
            pltpu.VMEM((3 * RANK, ROWS + 3 * OWN), BF16),
            pltpu.VMEM((RANK, 6 * RANK), BF16),
            pltpu.VMEM((OWN, 6 * RANK), BF16),
            reduce_buffers(ROWS, False),
            reduce_buffers(WIDE, True),
            dma((10,)),
            dma((2, 2, 2)),
            dma((13,)),
            dma((13,)),
            dma((2, N_CHUNK)),
            dma((2, N_CHUNK)),
            dma((2, N_CHUNK + 1)),
            dma((2, N_CHUNK + 1)),
            (dma((25,)), dma((25,))),
            (dma((25,)), dma((25,))),
            pltpu.SemaphoreType.REGULAR,
            pltpu.SemaphoreType.REGULAR,
        ],
        compiler_params=pltpu.CompilerParams(
            collective_id=0, has_side_effects=True, vmem_limit_bytes=48 << 20
        ),
        cost_estimate=pl.CostEstimate(
            flops=1 << 31, bytes_accessed=14 << 20, transcendentals=0
        ),
    )(grads, error, pltpu.with_memory_space_constraint(q_factor, pltpu.HBM))
    return pl.pallas_call(
        out_kernel,
        out_shape=(
            jax.ShapeDtypeStruct((OWN, COLS), F32),
            jax.ShapeDtypeStruct((1, OWN, COLS), F32),
            jax.ShapeDtypeStruct((RANK, COLS), F32),
        ),
        in_specs=[vmem] * 3,
        out_specs=(any_space,) * 3,
        scratch_shapes=[dma((1 + 2 * N_PART,))],
        compiler_params=pltpu.CompilerParams(vmem_limit_bytes=16 << 20),
    )(*results)


def solution(mesh):
    in_specs = (P("rep", "shard", None, None), P("rep", "shard", None), P())
    out_specs = (P("shard", None), P("rep", "shard", None), P())
    return jax.shard_map(body, mesh=mesh, in_specs=in_specs, out_specs=out_specs, check_vma=False)
```

```python
import functools

import jax
import jax.numpy as jnp
from jax import lax
from jax.experimental import pallas as pl
from jax.experimental.pallas import tpu as pltpu
from jax.sharding import PartitionSpec as P

MESH = pl.DeviceIdType.MESH
F32 = jnp.float32
BF16 = jnp.bfloat16
HIGHEST = lax.Precision.HIGHEST
ROWS, COLS, RANK = 1024, 3968, 32
NX, NY, NZ = 4, 4, 8
OWN = 128
HALF = OWN // 2
CHUNK = 16
WIDE = 4096
NT = (((1,), (1,)), ((), ()))
NN = (((1,), (0,)), ((), ()))


def split(value):
    high = value.astype(BF16)
    rest = value - high.astype(F32)
    middle = rest.astype(BF16)
    low = (rest - middle.astype(F32)).astype(BF16)
    return high, middle, low


def split3(value):
    return jnp.concatenate(split(value), axis=0)


def left6(value):
    high, middle, low = (term.astype(F32) for term in split(value))
    return jnp.concatenate([high, high, middle, high, low, middle], axis=0).T.astype(BF16)


def right6(value):
    high, middle, low = split(value)
    return jnp.concatenate([high, middle, high, low, high, middle], axis=0)


def fold3(value):
    return value[:RANK] + value[RANK : 2 * RANK] + value[2 * RANK : 3 * RANK]


def inverse_lower(gram):
    row = lax.broadcasted_iota(jnp.int32, (RANK, 2 * RANK), 0)
    col = lax.broadcasted_iota(jnp.int32, (RANK, 2 * RANK), 1)
    work = jnp.concatenate([gram, jnp.zeros((RANK, RANK), F32)], axis=1)
    work = jnp.where(col == row + RANK, 1.0, work)
    scale = jnp.zeros((RANK, 1), F32)
    row1 = lax.broadcasted_iota(jnp.int32, (RANK, 1), 0)
    for j in range(RANK):
        pivot_row = work[j : j + 1, :]
        pivot = work[j : j + 1, j : j + 1]
        factor = jnp.where(row1 > j, work[:, j : j + 1] / pivot, 0.0)
        scale = jnp.where(row1 == j, 1.0 / jnp.sqrt(pivot), scale)
        work = work - factor * pivot_row
    return work[:, RANK:] * scale


def main_kernel(
    g_hbm, e_hbm, q_hbm,
    approx, new_error, q_next,
    g, err, q, qs, psend, precv, far, near, fs, linv6, basis6,
    bufs_f, bufs_u,
    load_sem, sent_sem, p_rs, f_rs, n_rs, ar_f, ar_u, reply, ring_reply, ring,
):
    rep, shard = lax.axis_index("rep"), lax.axis_index("shard")
    x, z = rep // NZ, rep % NZ
    y, c = shard // 2, shard % 2

    def dev(dx, dy, dz, dc):
        return (
            ((x + dx) % NX) * NZ + (z + dz) % NZ,
            ((y + dy) % NY) * 2 + (c + dc) % 2,
        )

    partner = dev(0, 0, 0, 1)
    up, down = dev(0, 1, 0, 0), dev(0, NY - 1, 0, 0)
    x_peers = [dev(j, 0, 0, 0) for j in range(1, NX)]
    z_peers = [dev(0, 0, j, 0) for j in range(1, NZ)]
    y_peers = [dev(2, j, 0, 0) for j in range(1, NY)]
    barrier = pltpu.get_barrier_semaphore()

    def signal(semaphore, peer):
        pl.semaphore_signal(semaphore, 1, device_id=peer, device_id_type=MESH)

    def place(at):
        return at + (at == 2) - (at == 3)

    def signal_ring(semaphore, above):
        for j, peer in ((1, up), (3, down)):
            pl.when((place((y + j) % NY) > place(y)) == above)(
                functools.partial(signal, semaphore, peer)
            )

    def signal_far(semaphore, above):
        for j, peer in enumerate(z_peers):
            pl.when((z + j + 1 < NZ) == above)(functools.partial(signal, semaphore, peer))
        for j, peer in enumerate(x_peers):
            pl.when((place((x + j + 1) % NX) > place(x)) == above)(functools.partial(signal, semaphore, peer))

    def send(src, dst, ss, rs, to):
        pltpu.make_async_remote_copy(
            src_ref=src, dst_ref=dst, send_sem=ss, recv_sem=rs,
            device_id=to, device_id_type=MESH,
        ).start()

    def wait(semaphore, like):
        pltpu.make_async_copy(like, like, semaphore).wait()

    to_partner_sent, far_sent, near_sent, sum_sent = (sent_sem.at[i] for i in range(4))

    def first_row(k, t):
        return pl.multiple_of(OWN * (2 * ((y + k) % NY) + (c + t) % 2), OWN)

    def at(k, t):
        return OWN * (2 * k + t)

    signal(barrier, partner)
    signal_ring(barrier, True)
    q_load = pltpu.make_async_copy(q_hbm, q, load_sem.at[0])
    e_load = pltpu.make_async_copy(e_hbm.at[0], err, load_sem.at[1])
    for t, start, rows in (
        (1, 0, CHUNK), (0, 0, CHUNK), (1, CHUNK, HALF - CHUNK), (0, CHUNK, HALF - CHUNK)
    ):
        for d in (0, 1):
            pltpu.make_async_copy(
                g_hbm.at[0, 0, pl.ds(first_row(2, t) + d * HALF + start, rows)],
                g.at[pl.ds(at(2, t) + d * HALF + start, rows)],
                load_sem.at[2 if (t, start) == (1, 0) else 3],
            ).start()
    signal_far(barrier, True)

    def widen(k, start, rows):
        def step(i, carry):
            at_row = pl.multiple_of(start + i * CHUNK, CHUNK)
            psend[k, pl.ds(at_row, CHUNK), :] = g[
                pl.ds(at(k, 1) + at_row, CHUNK), :
            ].astype(F32)
            return carry

        lax.fori_loop(0, rows // CHUNK, step, 0)

    def to_partner(k, start, rows, i):
        window = (k, pl.ds(start, rows))
        send(psend.at[window], precv.at[window], to_partner_sent, p_rs.at[i], partner)

    def add_own(k, start, rows):
        def step(i, carry):
            at_row = pl.multiple_of(start + i * CHUNK, CHUNK)
            precv[k, pl.ds(at_row, CHUNK), :] += g[
                pl.ds(at(k, 0) + at_row, CHUNK), :
            ].astype(F32)
            return carry

        lax.fori_loop(0, rows // CHUNK, step, 0)

    wait(load_sem.at[2], g.at[pl.ds(at(2, 1), 2 * CHUNK)])
    for d in (0, 1):
        widen(2, d * HALF, CHUNK)
    q_load.start()
    e_load.start()
    for k in (1, 3, 0):
        for t in (1, 0):
            pltpu.make_async_copy(
                g_hbm.at[0, 0, pl.ds(first_row(k, t), OWN)],
                g.at[pl.ds(at(k, t), OWN)],
                load_sem.at[4],
            ).start()
    below = jnp.minimum(y, NY - y)
    pl.semaphore_wait(barrier, 1 + below + z + place(x))
    signal_ring(ring_reply, False)

    pieces = [(d, start, rows) for start, rows in ((0, CHUNK), (CHUNK, HALF - CHUNK)) for d in (0, 1)]
    for i, (d, start, rows) in enumerate(pieces):
        if i == 2:
            wait(load_sem.at[3], g.at[pl.ds(at(2, 0), 2 * OWN - 2 * CHUNK)])
            for e in (0, 1):
                widen(2, e * HALF + CHUNK, HALF - CHUNK)
        to_partner(2, d * HALF + start, rows, i)
    for i, (d, start, rows) in enumerate(pieces):
        here = pl.ds(d * HALF + start, rows)
        wait(p_rs.at[i], precv.at[2, here])
        add_own(2, d * HALF + start, rows)
        if i == 0:

            @pl.when(below < 2)
            def _():
                pl.semaphore_wait(ring_reply, 2 - below)

        send(precv.at[2, here], far.at[d, pl.ds(start, rows)], far_sent, f_rs.at[0], (up, down)[d])
    signal_far(reply, False)
    for peer in (up, down):
        signal(ring, peer)

    q_load.wait()
    qs[pl.ds(0, 3 * RANK), :] = split3(q[...])
    qs[pl.ds(3 * RANK, RANK), :] = jnp.zeros((RANK, COLS), BF16)
    e_load.wait()

    def split_error(i, carry):
        at_row = pl.multiple_of(i * CHUNK, CHUNK)
        for j, term in enumerate(split(err[pl.ds(at_row, CHUNK), :])):
            g[pl.ds(ROWS + j * OWN + at_row, CHUNK), :] = term
        return carry

    lax.fori_loop(0, OWN // CHUNK, split_error, 0)
    wait(load_sem.at[4], g.at[pl.ds(0, 3 * 2 * OWN)])
    def send_near(d, start, rows, i):
        send(
            precv.at[(1, 3)[d], pl.ds(start, rows)],
            near.at[d, pl.ds(start, rows)],
            near_sent, n_rs.at[i], (up, down)[d],
        )

    def widen_early():
        widen(1, HALF, HALF)
        to_partner(1, HALF, HALF, 4)
        widen(3, 0, HALF)
        to_partner(3, 0, HALF, 4)

    def near_early():
        wait(p_rs.at[4], precv.at[0])
        add_own(1, HALF, HALF)
        send_near(0, HALF, HALF, 0)
        add_own(3, 0, HALF)
        send_near(1, 0, HALF, 0)

    def widen_rest():
        widen(1, 0, HALF)
        to_partner(1, 0, HALF, 5)
        widen(3, HALF, HALF)
        to_partner(3, HALF, HALF, 5)
        widen(0, 0, OWN)
        to_partner(0, 0, OWN, 5)

    def near_late():
        wait(p_rs.at[5], precv.at[pl.ds(0, 2)])
        wait(f_rs.at[0], far)
        for i, (first, rows) in enumerate(((0, HALF - CHUNK), (HALF - CHUNK, CHUNK))):
            for d, k, half in ((0, 1, 0), (1, 3, HALF)):

                def step(j, carry, d=d, k=k, half=half, first=first):
                    at_row = pl.multiple_of(first + j * CHUNK, CHUNK)
                    here = pl.ds(half + at_row, CHUNK)
                    precv[k, here, :] = (
                        precv[k, here, :]
                        + g[pl.ds(at(k, 0) + half + at_row, CHUNK), :].astype(F32)
                        + far[d, pl.ds(at_row, CHUNK), :]
                    )
                    return carry

                lax.fori_loop(0, rows // CHUNK, step, 0)
                send_near(d, half + first, rows, 1 + i)

    def add_near(d, start, rows):
        def step(j, carry):
            here = pl.ds(pl.multiple_of(start + j * CHUNK, CHUNK), CHUNK)
            new_error[here, :] += near[d, here, :]
            return carry

        lax.fori_loop(0, rows // CHUNK, step, 0)

    def merge_own():
        def step(i, carry):
            here = pl.ds(pl.multiple_of(i * CHUNK, CHUNK), CHUNK)
            new_error[here, :] = (
                precv[0, here, :] + g[here, :].astype(F32) + err[here, :]
            )
            return carry

        lax.fori_loop(0, OWN // CHUNK, step, 0)

    def merge_early():
        wait(n_rs.at[0], near.at[0])
        add_near(0, HALF, HALF)
        add_near(1, 0, HALF)

    def all_reduce(width, bufs, sems, beside):
        part, core_in, z_in, x_all, x_sum, y_all, full = bufs
        piece = width // NZ
        mine = pl.multiple_of(16 * c, 16)
        theirs = pl.multiple_of(16 * (1 - c), 16)
        at_z = pl.multiple_of(piece * z, 128)

        def phase(name, i, copies, like):
            for src, dst, peer in copies:
                send(src, dst, sum_sent, sems.at[i], peer)
            beside(name)
            wait(sems.at[i], like)
            wait(sum_sent, like)

        phase("core", 0, [(part.at[pl.ds(theirs, 16)], core_in, partner)], core_in)
        core_in[...] += part[pl.ds(mine, 16), :]

        def there(j):
            return pl.ds(pl.multiple_of(piece * ((z + j + 1) % NZ), 128), piece)

        phase(
            "z", 1, [(core_in.at[:, there(j)], z_in.at[j], peer) for j, peer in enumerate(z_peers)], z_in
        )
        total = core_in[:, pl.ds(at_z, piece)]
        for j in range(NZ - 1):
            total = total + z_in[j]
        x_all[x] = total
        phase(
            "x", 2, [(x_all.at[x], x_all.at[x], peer) for peer in x_peers], x_all.at[pl.ds(0, NX - 1)]
        )
        total = (x_all[0] + x_all[1]) + (x_all[2] + x_all[3])
        quartered = y_all.shape[-1] < piece
        if quartered:
            quarter = piece // NX
            x_sum[...] = total
            y_all[y] = x_sum[:, pl.ds(pl.multiple_of(quarter * x, 128), quarter)]
            source = x_sum.at[:, pl.ds(pl.multiple_of(quarter * ((x + 2) % NX), 128), quarter)]
            window = (pl.ds(mine, 16), pl.ds(pl.multiple_of(at_z + quarter * x, 128), quarter))
        else:
            y_all[y] = total
            source = y_all.at[y]
            window = (pl.ds(mine, 16), pl.ds(at_z, piece))
        three = y_all.at[pl.ds(0, NY - 1)]
        phase("y", 3, [(source, y_all.at[y], peer) for peer in y_peers], three)
        full[window] = (y_all[0] + y_all[1]) + (y_all[2] + y_all[3])
        if quartered:
            phase("x2", 4, [(full.at[window], full.at[window], peer) for peer in x_peers], three)
            window = (pl.ds(mine, 16), pl.ds(at_z, piece))
        phase("z2", 5, [(full.at[window], full.at[window], peer) for peer in z_peers], z_in)
        window = (pl.ds(mine, 16),)
        phase("core2", 6, [(full.at[window], full.at[window], partner)], core_in)

    part_f = bufs_f[0]

    def left_terms(start, rows):
        terms = lax.dot_general(
            g[pl.ds(start, rows), :], qs[...], NT, preferred_element_type=F32
        )
        return fold3(terms.T)

    for k in (1, 2, 3):
        terms = left_terms(at(k, 0), 2 * OWN)
        for t in (0, 1):
            part_f[:, pl.ds(first_row(k, t), OWN)] = terms[:, OWN * t : OWN * (t + 1)]
    terms = left_terms(0, 2 * OWN)
    own = left_terms(ROWS, 3 * OWN)
    part_f[:, pl.ds(first_row(0, 1), OWN)] = terms[:, OWN:]
    part_f[:, pl.ds(first_row(0, 0), OWN)] = (
        terms[:, :OWN] + own[:, :OWN] + own[:, OWN : 2 * OWN] + own[:, 2 * OWN :]
    )

    def beside_f(phase):
        if phase == "core":
            pl.semaphore_wait(ring, 2)
            answers = (NZ - 1 - z) + (NX - 1 - place(x))

            @pl.when(answers > 0)
            def _():
                pl.semaphore_wait(reply, answers)

        elif phase == "z":
            widen_early()
        elif phase == "x":
            near_early()
        elif phase == "y":
            widen_rest()
        elif phase == "z2":
            near_late()

    all_reduce(ROWS, bufs_f, ar_f, beside_f)
    factor = bufs_f[6]

    for k in range(NY):
        for t in (0, 1):
            fs[:, pl.ds(at(k, t), OWN)] = split3(factor[:, pl.ds(first_row(k, t), OWN)])
    own_factor = factor[:, pl.ds(first_row(0, 0), OWN)]
    for j in range(3):
        fs[:, pl.ds(ROWS + j * OWN, OWN)] = split3(own_factor)
    part_u = bufs_u[0]
    for start in range(0, COLS, 1024):
        cols = pl.ds(start, min(1024, COLS - start))
        part_u[:, cols] = fold3(
            lax.dot_general(fs[...], g[:, cols], NN, preferred_element_type=F32)
        )
    part_u[:, pl.ds(COLS, WIDE - COLS)] = jnp.zeros((RANK, WIDE - COLS), F32)

    def beside_u(phase):
        if phase == "z":
            merge_own()
            whole = factor[...]
            gram = lax.dot_general(whole, whole, NT, precision=HIGHEST, preferred_element_type=F32)
            linv = inverse_lower(gram)
            linv6[...] = left6((linv * (1.0 / (NX * NZ))).T)
            basis = lax.dot_general(
                linv, own_factor, NN, precision=HIGHEST, preferred_element_type=F32
            )
            basis6[...] = left6(basis)
        elif phase == "z2":
            merge_early()

    all_reduce(WIDE, bufs_u, ar_u, beside_u)
    for start in range(0, COLS, 1024):
        cols = pl.ds(start, min(1024, COLS - start))
        right = lax.dot_general(
            linv6[...], right6(bufs_u[6][:, cols]), NN, preferred_element_type=F32
        )
        q_next[:, cols] = right
        value = lax.dot_general(basis6[...], right6(right), NN, preferred_element_type=F32)
        approx[:, cols] = value
        new_error[:, cols] -= value
    wait(to_partner_sent, psend)
    wait(far_sent, far)
    for i, first, rows in ((1, 0, HALF - CHUNK), (2, HALF - CHUNK, CHUNK)):
        wait(n_rs.at[i], near.at[0, pl.ds(0, 2 * rows)])
        add_near(0, first, rows)
        add_near(1, HALF + first, rows)
    wait(near_sent, near)


def reduce_buffers(width, quartered):
    piece = width // NZ
    return (
        pltpu.VMEM((RANK, width), F32),
        pltpu.VMEM((16, width), F32),
        pltpu.VMEM((NZ - 1, 16, piece), F32),
        pltpu.VMEM((NX, 16, piece), F32),
        pltpu.VMEM((16, piece), F32),
        pltpu.VMEM((NY, 16, piece // NX if quartered else piece), F32),
        pltpu.VMEM((RANK, width), F32),
    )


def out_kernel(approx, new_error, q_next, approx_out, new_error_out, q_out, sem):
    copies = [
        pltpu.make_async_copy(approx, approx_out, sem.at[0]),
        pltpu.make_async_copy(new_error, new_error_out.at[0], sem.at[1]),
        pltpu.make_async_copy(q_next, q_out, sem.at[2]),
    ]
    for copy in copies:
        copy.start()
    for copy in copies:
        copy.wait()


def body(grads, error, q_factor):
    any_space = pl.BlockSpec(memory_space=pl.ANY)
    vmem = pl.BlockSpec(memory_space=pltpu.VMEM)
    dma = pltpu.SemaphoreType.DMA
    results = pl.pallas_call(
        main_kernel,
        out_shape=(
            pltpu.VMEM((OWN, COLS), F32),
            pltpu.VMEM((OWN, COLS), F32),
            pltpu.VMEM((RANK, COLS), F32),
        ),
        in_specs=[any_space] * 3,
        out_specs=(vmem,) * 3,
        scratch_shapes=[
            pltpu.VMEM((ROWS + 3 * OWN, COLS), BF16),
            pltpu.VMEM((OWN, COLS), F32),
            pltpu.VMEM((RANK, COLS), F32),
            pltpu.VMEM((4 * RANK, COLS), BF16),
            pltpu.VMEM((NY, OWN, COLS), F32),
            pltpu.VMEM((NY, OWN, COLS), F32),
            pltpu.VMEM((2, HALF, COLS), F32),
            pltpu.VMEM((2, OWN, COLS), F32),
            pltpu.VMEM((3 * RANK, ROWS + 3 * OWN), BF16),
            pltpu.VMEM((RANK, 6 * RANK), BF16),
            pltpu.VMEM((OWN, 6 * RANK), BF16),
            reduce_buffers(ROWS, False),
            reduce_buffers(WIDE, True),
            dma((5,)),
            dma((4,)),
            dma((6,)),
            dma((1,)),
            dma((3,)),
            dma((7,)),
            dma((7,)),
            pltpu.SemaphoreType.REGULAR,
            pltpu.SemaphoreType.REGULAR,
            pltpu.SemaphoreType.REGULAR,
        ],
        compiler_params=pltpu.CompilerParams(
            collective_id=0, has_side_effects=True, vmem_limit_bytes=48 << 20
        ),
        cost_estimate=pl.CostEstimate(
            flops=1 << 31, bytes_accessed=14 << 20, transcendentals=0
        ),
    )(grads, error, pltpu.with_memory_space_constraint(q_factor, pltpu.HBM))
    return pl.pallas_call(
        out_kernel,
        out_shape=(
            jax.ShapeDtypeStruct((OWN, COLS), F32),
            jax.ShapeDtypeStruct((1, OWN, COLS), F32),
            jax.ShapeDtypeStruct((RANK, COLS), F32),
        ),
        in_specs=[vmem] * 3,
        out_specs=(any_space,) * 3,
        scratch_shapes=[dma((3,))],
        compiler_params=pltpu.CompilerParams(vmem_limit_bytes=16 << 20),
    )(*results)


def solution(mesh):
    in_specs = (P("rep", "shard", None, None), P("rep", "shard", None), P())
    out_specs = (P("shard", None), P("rep", "shard", None), P())
    return jax.shard_map(body, mesh=mesh, in_specs=in_specs, out_specs=out_specs, check_vma=False)
```

```python
import functools

import jax
import jax.numpy as jnp
from jax import lax
from jax.experimental import pallas as pl
from jax.experimental.pallas import tpu as pltpu
from jax.sharding import PartitionSpec as P

MESH = pl.DeviceIdType.MESH
F32 = jnp.float32
BF16 = jnp.bfloat16
HIGHEST = lax.Precision.HIGHEST
ROWS, COLS, RANK = 1024, 3968, 32
NX, NY, NZ = 4, 4, 8
OWN = 128
HALF = OWN // 2
CHUNK = 16
FIRST = 1024
LAST = ((0, HALF - 8), (HALF - 8, 8))
CORNER = 640
FULL = COLS - CORNER
CORNER_ROWS = (HALF - CHUNK, HALF)
WIDE = 4096
NT = (((1,), (1,)), ((), ()))
NN = (((1,), (0,)), ((), ()))


def split(value):
    high = value.astype(BF16)
    rest = value - high.astype(F32)
    middle = rest.astype(BF16)
    low = (rest - middle.astype(F32)).astype(BF16)
    return high, middle, low


def split3(value):
    return jnp.concatenate(split(value), axis=0)


def left6(value):
    high, middle, low = (term.astype(F32) for term in split(value))
    return jnp.concatenate([high, high, middle, high, low, middle], axis=0).T.astype(BF16)


def right6(value):
    high, middle, low = split(value)
    return jnp.concatenate([high, middle, high, low, high, middle], axis=0)


def fold3(value):
    return value[:RANK] + value[RANK : 2 * RANK] + value[2 * RANK : 3 * RANK]


def inverse_lower(gram):
    row = lax.broadcasted_iota(jnp.int32, (RANK, 2 * RANK), 0)
    col = lax.broadcasted_iota(jnp.int32, (RANK, 2 * RANK), 1)
    work = jnp.concatenate([gram, jnp.zeros((RANK, RANK), F32)], axis=1)
    work = jnp.where(col == row + RANK, 1.0, work)
    scale = jnp.zeros((RANK, 1), F32)
    row1 = lax.broadcasted_iota(jnp.int32, (RANK, 1), 0)
    for j in range(RANK):
        pivot_row = work[j : j + 1, :]
        pivot = work[j : j + 1, j : j + 1]
        factor = jnp.where(row1 > j, work[:, j : j + 1] / pivot, 0.0)
        scale = jnp.where(row1 == j, 1.0 / jnp.sqrt(pivot), scale)
        work = work - factor * pivot_row
    return work[:, RANK:] * scale


def main_kernel(
    g_hbm, e_hbm, q_hbm,
    approx, new_error, q_next,
    g, err, q, qs, psend, precv, far, corner, near, fs, linv6, basis6,
    bufs_f, bufs_u,
    load_sem, sent_sem, p_rs, f_rs, n_rs, ar_f, ar_u, reply, ring_reply, ring,
):
    rep, shard = lax.axis_index("rep"), lax.axis_index("shard")
    x, z = rep // NZ, rep % NZ
    y, c = shard // 2, shard % 2

    def dev(dx, dy, dz, dc):
        return (
            ((x + dx) % NX) * NZ + (z + dz) % NZ,
            ((y + dy) % NY) * 2 + (c + dc) % 2,
        )

    partner = dev(0, 0, 0, 1)
    up, down = dev(0, 1, 0, 0), dev(0, NY - 1, 0, 0)
    x_peers = [dev(j, 0, 0, 0) for j in range(1, NX)]
    z_peers = [dev(0, 0, j, 0) for j in range(1, NZ)]
    y_peers = [dev(2, j, 0, 0) for j in range(1, NY)]
    barrier = pltpu.get_barrier_semaphore()

    def signal(semaphore, peer):
        pl.semaphore_signal(semaphore, 1, device_id=peer, device_id_type=MESH)

    def place(at):
        return at + (at == 2) - (at == 3)

    def signal_ring(semaphore, above):
        for j, peer in ((1, up), (3, down)):
            pl.when((place((y + j) % NY) > place(y)) == above)(
                functools.partial(signal, semaphore, peer)
            )

    def signal_far(semaphore, above):
        for j, peer in enumerate(z_peers):
            pl.when((z + j + 1 < NZ) == above)(functools.partial(signal, semaphore, peer))
        for j, peer in enumerate(x_peers):
            pl.when((place((x + j + 1) % NX) > place(x)) == above)(functools.partial(signal, semaphore, peer))

    def send(src, dst, ss, rs, to):
        pltpu.make_async_remote_copy(
            src_ref=src, dst_ref=dst, send_sem=ss, recv_sem=rs,
            device_id=to, device_id_type=MESH,
        ).start()

    def wait(semaphore, like):
        pltpu.make_async_copy(like, like, semaphore).wait()

    but_corners = psend.at[pl.ds(0, 2), pl.ds(0, 112), pl.ds(0, 17 * 128)]

    to_partner_sent, far_sent, corner_sent, near_sent, sum_sent = (sent_sem.at[i] for i in range(5))

    def first_row(k, t):
        return pl.multiple_of(OWN * (2 * ((y + k) % NY) + (c + t) % 2), OWN)

    def at(k, t):
        return OWN * (2 * k + t)

    signal(barrier, partner)
    corner[...] = jnp.zeros(corner.shape, F32)
    for d in (0, 1):
        far[d, pl.ds((1 - d) * (HALF - CHUNK), CHUNK), pl.ds(FULL, CORNER)] = jnp.zeros(
            (CHUNK, CORNER), F32
        )
    signal_ring(barrier, True)
    q_load = pltpu.make_async_copy(q_hbm, q, load_sem.at[0])
    e_load = pltpu.make_async_copy(e_hbm.at[0], err, load_sem.at[1])
    def load_far(t, start, rows, i):
        for d in (0, 1):
            pltpu.make_async_copy(
                g_hbm.at[0, 0, pl.ds(first_row(2, t) + d * HALF + start, rows)],
                g.at[pl.ds(at(2, t) + d * HALF + start, rows)],
                load_sem.at[i],
            ).start()

    load_far(1, 0, CHUNK, 2)
    signal_far(barrier, True)
    load_far(0, 0, CHUNK, 3)
    load_far(1, CHUNK, HALF - CHUNK, 3)
    load_far(0, CHUNK, HALF - CHUNK, 3)

    def widen(k, start, rows):
        def step(i, carry):
            at_row = pl.multiple_of(start + i * CHUNK, CHUNK)
            psend[k, pl.ds(at_row, CHUNK), :] = g[
                pl.ds(at(k, 1) + at_row, CHUNK), :
            ].astype(F32)
            return carry

        lax.fori_loop(0, rows // CHUNK, step, 0)

    def to_partner(k, start, rows, i, cols=slice(None)):
        window = (k, pl.ds(start, rows), cols)
        send(psend.at[window], precv.at[window], to_partner_sent, p_rs.at[i], partner)

    def add_own(k, start, rows, cols=slice(None)):
        def step(i, carry):
            at_row = pl.multiple_of(start + i * CHUNK, CHUNK)
            precv[k, pl.ds(at_row, CHUNK), cols] += g[
                pl.ds(at(k, 0) + at_row, CHUNK), cols
            ].astype(F32)
            return carry

        lax.fori_loop(0, rows // CHUNK, step, 0)

    wait(load_sem.at[2], g.at[pl.ds(at(2, 1), 2 * CHUNK)])
    for d in (0, 1):
        widen(2, d * HALF, CHUNK)
    q_load.start()
    e_load.start()
    for k in (1, 3, 0):
        for t in (1, 0):
            pltpu.make_async_copy(
                g_hbm.at[0, 0, pl.ds(first_row(k, t), OWN)],
                g.at[pl.ds(at(k, t), OWN)],
                load_sem.at[4],
            ).start()
    below = jnp.minimum(y, NY - y)
    pl.semaphore_wait(barrier, 1 + below + z + place(x))
    signal_ring(ring_reply, False)

    few, most, every = pl.ds(0, FIRST), pl.ds(FIRST, COLS - FIRST), pl.ds(0, COLS)
    pieces = [
        (d, start, rows, cols)
        for start, rows, cols in (
            (0, CHUNK, few), (0, CHUNK, most), (CHUNK, HALF - CHUNK, every)
        )
        for d in (0, 1)
    ]
    tails = [pl.ds(FULL, CORNER), pl.ds(0, FULL)]
    own_way = {
        3: [(0, CHUNK, pl.ds(FIRST, FULL - FIRST))],
        4: [(CHUNK, HALF - 2 * CHUNK, every), (HALF - CHUNK, CHUNK, tails[1])],
    }
    for i, (d, start, rows, cols) in enumerate(pieces):
        if i == 4:
            wait(load_sem.at[3], g.at[pl.ds(at(2, 0), 2 * OWN - 2 * CHUNK)])
            for e in (0, 1):
                widen(2, e * HALF + CHUNK, HALF - CHUNK)
        to_partner(2, d * HALF + start, rows, i, cols)
    for i, (d, start, rows, cols) in enumerate(pieces):
        here = (2, pl.ds(d * HALF + start, rows), cols)
        wait(p_rs.at[i], precv.at[here])
        add_own(2, d * HALF + start, rows, cols)
        if i == 0:

            @pl.when(below < 2)
            def _():
                pl.semaphore_wait(ring_reply, 2 - below)

        for start, rows, cols in own_way.get(i, [(start, rows, cols)]):
            send(
                precv.at[2, pl.ds(d * HALF + start, rows), cols],
                far.at[d, pl.ds(start, rows), cols], far_sent, f_rs.at[0], (up, down)[d],
            )
    for r, odd in ((0, 3), (1, 1)):
        source = precv.at[2, pl.ds(CORNER_ROWS[r], CHUNK), tails[0]]
        for way in (0, 1):

            @pl.when((y == odd) == (way != r))
            def _(r=r, way=way, source=source):
                send(source, corner.at[way, r], corner_sent, f_rs.at[1], (up, down)[way])

    signal_far(reply, False)
    for peer in (up, down):
        signal(ring, peer)

    q_load.wait()
    qs[pl.ds(0, 3 * RANK), :] = split3(q[...])
    qs[pl.ds(3 * RANK, RANK), :] = jnp.zeros((RANK, COLS), BF16)
    e_load.wait()

    def split_error(i, carry):
        at_row = pl.multiple_of(i * CHUNK, CHUNK)
        for j, term in enumerate(split(err[pl.ds(at_row, CHUNK), :])):
            g[pl.ds(ROWS + j * OWN + at_row, CHUNK), :] = term
        return carry

    lax.fori_loop(0, OWN // CHUNK, split_error, 0)
    wait(load_sem.at[4], g.at[pl.ds(0, 3 * 2 * OWN)])
    def send_near(d, start, rows, i, cols=slice(None)):
        window = (pl.ds(start, rows), cols)
        send(
            precv.at[((1, 3)[d], *window)],
            near.at[(d, *window)],
            near_sent, n_rs.at[i], (up, down)[d],
        )

    def widen_early():
        widen(1, HALF, HALF)
        to_partner(1, HALF, HALF, 6)
        widen(3, 0, HALF)
        to_partner(3, 0, HALF, 6)

    def near_early():
        wait(p_rs.at[6], precv.at[0])
        add_own(1, HALF, HALF)
        send_near(0, HALF + CHUNK, HALF - CHUNK, 0)
        send_near(0, HALF, CHUNK, 0, tails[1])
        add_own(3, 0, HALF)
        send_near(1, 0, HALF - CHUNK, 0)
        send_near(1, HALF - CHUNK, CHUNK, 0, tails[1])

    def widen_rest():
        widen(1, 0, HALF)
        to_partner(1, 0, HALF, 7)
        widen(3, HALF, HALF)
        to_partner(3, HALF, HALF, 7)
        widen(0, 0, OWN)
        to_partner(0, 0, OWN, 7)

    def near_late():
        wait(p_rs.at[7], precv.at[pl.ds(0, 2)])
        wait(f_rs.at[0], but_corners)

        @pl.when(y % 2 == 1)
        def _():
            wait(f_rs.at[1], corner.at[0])

        @pl.when(y == 2)
        def _():
            wait(f_rs.at[1], corner)

        for d, k in ((0, 1), (1, 3)):
            for r in (0, 1):
                here = (k, pl.ds(CORNER_ROWS[r], CHUNK), tails[0])
                precv[here] += corner[d, r]
            send_near(d, CORNER_ROWS[1 - d], CHUNK, 3, tails[0])
        for d, k, half in ((0, 1, 0), (1, 3, HALF)):

            def step(j, carry, d=d, k=k, half=half):
                at_row = pl.multiple_of(j * CHUNK, CHUNK)
                here = pl.ds(half + at_row, CHUNK)
                precv[k, here, :] = (
                    precv[k, here, :]
                    + g[pl.ds(at(k, 0) + half + at_row, CHUNK), :].astype(F32)
                    + far[d, pl.ds(at_row, CHUNK), :]
                )
                return carry

            lax.fori_loop(0, HALF // CHUNK, step, 0)
        for i, (first, rows) in enumerate(LAST):
            for d, half in ((0, 0), (1, HALF)):
                send_near(d, half + first, rows, 1 + i)

    def add_near(d, start, rows):
        def step(j, carry):
            here = pl.ds(pl.multiple_of(start + j * 8, 8), 8)
            new_error[here, :] += near[d, here, :]
            return carry

        lax.fori_loop(0, rows // 8, step, 0)

    def merge_own():
        def step(i, carry):
            here = pl.ds(pl.multiple_of(i * CHUNK, CHUNK), CHUNK)
            new_error[here, :] = (
                precv[0, here, :] + g[here, :].astype(F32) + err[here, :]
            )
            return carry

        lax.fori_loop(0, OWN // CHUNK, step, 0)

    def merge_early():
        wait(n_rs.at[0], but_corners)
        wait(n_rs.at[3], corner.at[0])
        add_near(0, HALF, HALF)
        add_near(1, 0, HALF)

    def all_reduce(width, bufs, sems, beside):
        part, core_in, z_in, x_all, x_sum, y_all, full = bufs
        piece = width // NZ
        mine = pl.multiple_of(16 * c, 16)
        theirs = pl.multiple_of(16 * (1 - c), 16)
        at_z = pl.multiple_of(piece * z, 128)

        def phase(name, i, copies, like):
            for src, dst, peer in copies:
                send(src, dst, sum_sent, sems.at[i], peer)
            beside(name)
            wait(sems.at[i], like)
            wait(sum_sent, like)

        phase("core", 0, [(part.at[pl.ds(theirs, 16)], core_in, partner)], core_in)
        core_in[...] += part[pl.ds(mine, 16), :]

        def there(j):
            return pl.ds(pl.multiple_of(piece * ((z + j + 1) % NZ), 128), piece)

        phase(
            "z", 1, [(core_in.at[:, there(j)], z_in.at[j], peer) for j, peer in enumerate(z_peers)], z_in
        )
        total = core_in[:, pl.ds(at_z, piece)]
        for j in range(NZ - 1):
            total = total + z_in[j]
        x_all[x] = total
        phase(
            "x", 2, [(x_all.at[x], x_all.at[x], peer) for peer in x_peers], x_all.at[pl.ds(0, NX - 1)]
        )
        total = (x_all[0] + x_all[1]) + (x_all[2] + x_all[3])
        quartered = y_all.shape[-1] < piece
        if quartered:
            quarter = piece // NX
            x_sum[...] = total
            y_all[y] = x_sum[:, pl.ds(pl.multiple_of(quarter * x, 128), quarter)]
            source = x_sum.at[:, pl.ds(pl.multiple_of(quarter * ((x + 2) % NX), 128), quarter)]
            window = (pl.ds(mine, 16), pl.ds(pl.multiple_of(at_z + quarter * x, 128), quarter))
        else:
            y_all[y] = total
            source = y_all.at[y]
            window = (pl.ds(mine, 16), pl.ds(at_z, piece))
        three = y_all.at[pl.ds(0, NY - 1)]
        phase("y", 3, [(source, y_all.at[y], peer) for peer in y_peers], three)
        full[window] = (y_all[0] + y_all[1]) + (y_all[2] + y_all[3])
        if quartered:
            phase("x2", 4, [(full.at[window], full.at[window], peer) for peer in x_peers], three)
            window = (pl.ds(mine, 16), pl.ds(at_z, piece))
        phase("z2", 5, [(full.at[window], full.at[window], peer) for peer in z_peers], z_in)
        window = (pl.ds(mine, 16),)
        phase("core2", 6, [(full.at[window], full.at[window], partner)], core_in)

    part_f = bufs_f[0]

    def left_terms(start, rows):
        terms = lax.dot_general(
            g[pl.ds(start, rows), :], qs[...], NT, preferred_element_type=F32
        )
        return fold3(terms.T)

    for k in (1, 2, 3):
        terms = left_terms(at(k, 0), 2 * OWN)
        for t in (0, 1):
            part_f[:, pl.ds(first_row(k, t), OWN)] = terms[:, OWN * t : OWN * (t + 1)]
    terms = left_terms(0, 2 * OWN)
    own = left_terms(ROWS, 3 * OWN)
    part_f[:, pl.ds(first_row(0, 1), OWN)] = terms[:, OWN:]
    part_f[:, pl.ds(first_row(0, 0), OWN)] = (
        terms[:, :OWN] + own[:, :OWN] + own[:, OWN : 2 * OWN] + own[:, 2 * OWN :]
    )

    def beside_f(phase):
        if phase == "core":
            pl.semaphore_wait(ring, 2)
            answers = (NZ - 1 - z) + (NX - 1 - place(x))

            @pl.when(answers > 0)
            def _():
                pl.semaphore_wait(reply, answers)

        elif phase == "z":
            widen_early()
        elif phase == "x":
            near_early()
        elif phase == "y":
            widen_rest()
        elif phase == "z2":
            near_late()

    all_reduce(ROWS, bufs_f, ar_f, beside_f)
    factor = bufs_f[6]

    for k in range(NY):
        for t in (0, 1):
            fs[:, pl.ds(at(k, t), OWN)] = split3(factor[:, pl.ds(first_row(k, t), OWN)])
    own_factor = factor[:, pl.ds(first_row(0, 0), OWN)]
    for j in range(3):
        fs[:, pl.ds(ROWS + j * OWN, OWN)] = split3(own_factor)
    part_u = bufs_u[0]
    for start in range(0, COLS, 1024):
        cols = pl.ds(start, min(1024, COLS - start))
        part_u[:, cols] = fold3(
            lax.dot_general(fs[...], g[:, cols], NN, preferred_element_type=F32)
        )
    part_u[:, pl.ds(COLS, WIDE - COLS)] = jnp.zeros((RANK, WIDE - COLS), F32)

    def beside_u(phase):
        if phase == "z":
            merge_own()
            whole = factor[...]
            gram = lax.dot_general(whole, whole, NT, precision=HIGHEST, preferred_element_type=F32)
            linv = inverse_lower(gram)
            linv6[...] = left6((linv * (1.0 / (NX * NZ))).T)
            basis = lax.dot_general(
                linv, own_factor, NN, precision=HIGHEST, preferred_element_type=F32
            )
            basis6[...] = left6(basis)
        elif phase == "z2":
            merge_early()

    all_reduce(WIDE, bufs_u, ar_u, beside_u)
    for start in range(0, COLS, 1024):
        cols = pl.ds(start, min(1024, COLS - start))
        right = lax.dot_general(
            linv6[...], right6(bufs_u[6][:, cols]), NN, preferred_element_type=F32
        )
        q_next[:, cols] = right
        value = lax.dot_general(basis6[...], right6(right), NN, preferred_element_type=F32)
        approx[:, cols] = value
        new_error[:, cols] -= value
    wait(to_partner_sent, psend)
    wait(far_sent, but_corners)
    wait(corner_sent, corner.at[0])
    for i, (first, rows) in enumerate(LAST):
        wait(n_rs.at[1 + i], near.at[0, pl.ds(0, 2 * rows)])
        add_near(0, first, rows)
        add_near(1, HALF + first, rows)
    wait(near_sent, near)


def reduce_buffers(width, quartered):
    piece = width // NZ
    return (
        pltpu.VMEM((RANK, width), F32),
        pltpu.VMEM((16, width), F32),
        pltpu.VMEM((NZ - 1, 16, piece), F32),
        pltpu.VMEM((NX, 16, piece), F32),
        pltpu.VMEM((16, piece), F32),
        pltpu.VMEM((NY, 16, piece // NX if quartered else piece), F32),
        pltpu.VMEM((RANK, width), F32),
    )


def out_kernel(approx, new_error, q_next, approx_out, new_error_out, q_out, sem):
    copies = [
        pltpu.make_async_copy(approx, approx_out, sem.at[0]),
        pltpu.make_async_copy(new_error, new_error_out.at[0], sem.at[1]),
        pltpu.make_async_copy(q_next, q_out, sem.at[2]),
    ]
    for copy in copies:
        copy.start()
    for copy in copies:
        copy.wait()


def body(grads, error, q_factor):
    any_space = pl.BlockSpec(memory_space=pl.ANY)
    vmem = pl.BlockSpec(memory_space=pltpu.VMEM)
    dma = pltpu.SemaphoreType.DMA
    results = pl.pallas_call(
        main_kernel,
        out_shape=(
            pltpu.VMEM((OWN, COLS), F32),
            pltpu.VMEM((OWN, COLS), F32),
            pltpu.VMEM((RANK, COLS), F32),
        ),
        in_specs=[any_space] * 3,
        out_specs=(vmem,) * 3,
        scratch_shapes=[
            pltpu.VMEM((ROWS + 3 * OWN, COLS), BF16),
            pltpu.VMEM((OWN, COLS), F32),
            pltpu.VMEM((RANK, COLS), F32),
            pltpu.VMEM((4 * RANK, COLS), BF16),
            pltpu.VMEM((NY, OWN, COLS), F32),
            pltpu.VMEM((NY, OWN, COLS), F32),
            pltpu.VMEM((2, HALF, COLS), F32),
            pltpu.VMEM((2, 2, CHUNK, CORNER), F32),
            pltpu.VMEM((2, OWN, COLS), F32),
            pltpu.VMEM((3 * RANK, ROWS + 3 * OWN), BF16),
            pltpu.VMEM((RANK, 6 * RANK), BF16),
            pltpu.VMEM((OWN, 6 * RANK), BF16),
            reduce_buffers(ROWS, False),
            reduce_buffers(WIDE, True),
            dma((5,)),
            dma((5,)),
            dma((8,)),
            dma((2,)),
            dma((4,)),
            dma((7,)),
            dma((7,)),
            pltpu.SemaphoreType.REGULAR,
            pltpu.SemaphoreType.REGULAR,
            pltpu.SemaphoreType.REGULAR,
        ],
        compiler_params=pltpu.CompilerParams(
            collective_id=0, has_side_effects=True, vmem_limit_bytes=48 << 20
        ),
        cost_estimate=pl.CostEstimate(
            flops=1 << 31, bytes_accessed=14 << 20, transcendentals=0
        ),
    )(grads, error, pltpu.with_memory_space_constraint(q_factor, pltpu.HBM))
    return pl.pallas_call(
        out_kernel,
        out_shape=(
            jax.ShapeDtypeStruct((OWN, COLS), F32),
            jax.ShapeDtypeStruct((1, OWN, COLS), F32),
            jax.ShapeDtypeStruct((RANK, COLS), F32),
        ),
        in_specs=[vmem] * 3,
        out_specs=(any_space,) * 3,
        scratch_shapes=[dma((3,))],
        compiler_params=pltpu.CompilerParams(vmem_limit_bytes=16 << 20),
    )(*results)


def solution(mesh):
    in_specs = (P("rep", "shard", None, None), P("rep", "shard", None), P())
    out_specs = (P("shard", None), P("rep", "shard", None), P())
    return jax.shard_map(body, mesh=mesh, in_specs=in_specs, out_specs=out_specs, check_vma=False)
```

```python
import functools

import jax
import jax.numpy as jnp
from jax import lax
from jax.experimental import pallas as pl
from jax.experimental.pallas import tpu as pltpu
from jax.sharding import PartitionSpec as P

MESH = pl.DeviceIdType.MESH
F32 = jnp.float32
BF16 = jnp.bfloat16
HIGHEST = lax.Precision.HIGHEST
ROWS, COLS, RANK = 1024, 3968, 32
NX, NY, NZ = 4, 4, 8
OWN = 128
HALF = OWN // 2
CHUNK = 16
FIRST = 1024
LAST = ((0, HALF - 8), (HALF - 8, 8))
CORNER = 640
FULL = COLS - CORNER
CORNER_ROWS = (HALF - CHUNK, HALF)
WIDE = 4096
NT = (((1,), (1,)), ((), ()))
NN = (((1,), (0,)), ((), ()))


def split(value):
    high = value.astype(BF16)
    rest = value - high.astype(F32)
    middle = rest.astype(BF16)
    low = (rest - middle.astype(F32)).astype(BF16)
    return high, middle, low


def split3(value):
    return jnp.concatenate(split(value), axis=0)


def left6(value):
    high, middle, low = (term.astype(F32) for term in split(value))
    return jnp.concatenate([high, high, middle, high, low, middle], axis=0).T.astype(BF16)


def right6(value):
    high, middle, low = split(value)
    return jnp.concatenate([high, middle, high, low, high, middle], axis=0)


def fold3(value):
    return value[:RANK] + value[RANK : 2 * RANK] + value[2 * RANK : 3 * RANK]


def inverse_lower(gram):
    row = lax.broadcasted_iota(jnp.int32, (RANK, 2 * RANK), 0)
    col = lax.broadcasted_iota(jnp.int32, (RANK, 2 * RANK), 1)
    work = jnp.concatenate([gram, jnp.zeros((RANK, RANK), F32)], axis=1)
    work = jnp.where(col == row + RANK, 1.0, work)
    scale = jnp.zeros((RANK, 1), F32)
    row1 = lax.broadcasted_iota(jnp.int32, (RANK, 1), 0)
    for j in range(RANK):
        pivot_row = work[j : j + 1, :]
        pivot = work[j : j + 1, j : j + 1]
        factor = jnp.where(row1 > j, work[:, j : j + 1] / pivot, 0.0)
        scale = jnp.where(row1 == j, 1.0 / jnp.sqrt(pivot), scale)
        work = work - factor * pivot_row
    return work[:, RANK:] * scale


def main_kernel(
    g_hbm, e_hbm, q_hbm,
    approx, new_error, q_next,
    g, err, q, qs, psend, precv, far, corner, near, fs, linv6, basis6,
    bufs_f, bufs_u,
    load_sem, sent_sem, p_rs, f_rs, n_rs, ar_f, ar_u, reply, known, ring_reply, ring,
):
    rep, shard = lax.axis_index("rep"), lax.axis_index("shard")
    x, z = rep // NZ, rep % NZ
    y, c = shard // 2, shard % 2

    def dev(dx, dy, dz, dc):
        return (
            ((x + dx) % NX) * NZ + (z + dz) % NZ,
            ((y + dy) % NY) * 2 + (c + dc) % 2,
        )

    partner = dev(0, 0, 0, 1)
    up, down = dev(0, 1, 0, 0), dev(0, NY - 1, 0, 0)
    x_peers = [dev(j, 0, 0, 0) for j in range(1, NX)]
    z_peers = [dev(0, 0, j, 0) for j in range(1, NZ)]
    y_peers = [dev(1, j, 0, 0) for j in range(1, NY)]
    barrier = pltpu.get_barrier_semaphore()

    def signal(semaphore, peer):
        pl.semaphore_signal(semaphore, 1, device_id=peer, device_id_type=MESH)

    def place(at):
        return at + (at == 2) - (at == 3)

    def signal_ring(semaphore, above):
        for j, peer in ((1, up), (3, down)):
            pl.when((place((y + j) % NY) > place(y)) == above)(
                functools.partial(signal, semaphore, peer)
            )

    def signal_far(semaphore, above):
        for j, peer in enumerate(z_peers):
            greets = (z + j + 1 < NZ) == above
            if j == 2:
                greets = greets & (z != 4)
            elif j == 3:
                greets = greets & (z % 4 != 3)
            elif j == 4:
                greets = greets & (z != NZ - 1)
            pl.when(greets)(functools.partial(signal, semaphore, peer))
        for j, peer in enumerate(x_peers):
            pl.when((place((x + j + 1) % NX) > place(x)) == above)(functools.partial(signal, semaphore, peer))

    def send(src, dst, ss, rs, to):
        pltpu.make_async_remote_copy(
            src_ref=src, dst_ref=dst, send_sem=ss, recv_sem=rs,
            device_id=to, device_id_type=MESH,
        ).start()

    def wait(semaphore, like):
        pltpu.make_async_copy(like, like, semaphore).wait()

    but_corners = psend.at[pl.ds(0, 2), pl.ds(0, 112), pl.ds(0, 17 * 128)]

    to_partner_sent, far_sent, corner_sent, near_sent, sum_sent = (sent_sem.at[i] for i in range(5))

    def first_row(k, t):
        return pl.multiple_of(OWN * (2 * ((y + k) % NY) + (c + t) % 2), OWN)

    def at(k, t):
        return OWN * (2 * k + t)

    signal(barrier, partner)
    corner[...] = jnp.zeros(corner.shape, F32)
    for d in (0, 1):
        far[d, pl.ds((1 - d) * (HALF - CHUNK), CHUNK), pl.ds(FULL, CORNER)] = jnp.zeros(
            (CHUNK, CORNER), F32
        )
    signal_ring(barrier, True)
    q_load = pltpu.make_async_copy(q_hbm, q, load_sem.at[0])
    e_load = pltpu.make_async_copy(e_hbm.at[0], err, load_sem.at[1])
    def load_far(t, start, rows, i):
        for d in (0, 1):
            pltpu.make_async_copy(
                g_hbm.at[0, 0, pl.ds(first_row(2, t) + d * HALF + start, rows)],
                g.at[pl.ds(at(2, t) + d * HALF + start, rows)],
                load_sem.at[i],
            ).start()

    load_far(1, 0, CHUNK, 2)
    signal_far(barrier, True)
    load_far(0, 0, CHUNK, 3)
    load_far(1, CHUNK, HALF - CHUNK, 3)
    load_far(0, CHUNK, HALF - CHUNK, 3)

    def widen(k, start, rows):
        def step(i, carry):
            at_row = pl.multiple_of(start + i * CHUNK, CHUNK)
            psend[k, pl.ds(at_row, CHUNK), :] = g[
                pl.ds(at(k, 1) + at_row, CHUNK), :
            ].astype(F32)
            return carry

        lax.fori_loop(0, rows // CHUNK, step, 0)

    def to_partner(k, start, rows, i, cols=slice(None)):
        window = (k, pl.ds(start, rows), cols)
        send(psend.at[window], precv.at[window], to_partner_sent, p_rs.at[i], partner)

    def add_own(k, start, rows, cols=slice(None)):
        def step(i, carry):
            at_row = pl.multiple_of(start + i * CHUNK, CHUNK)
            precv[k, pl.ds(at_row, CHUNK), cols] += g[
                pl.ds(at(k, 0) + at_row, CHUNK), cols
            ].astype(F32)
            return carry

        lax.fori_loop(0, rows // CHUNK, step, 0)

    wait(load_sem.at[2], g.at[pl.ds(at(2, 1), 2 * CHUNK)])
    for d in (0, 1):
        widen(2, d * HALF, CHUNK)
    q_load.start()
    e_load.start()
    for k in (1, 3, 0):
        for t in (1, 0):
            pltpu.make_async_copy(
                g_hbm.at[0, 0, pl.ds(first_row(k, t), OWN)],
                g.at[pl.ds(at(k, t), OWN)],
                load_sem.at[4],
            ).start()
    below = jnp.minimum(y, NY - y)
    below_z = z - 2 * (z // (NZ - 1))
    pl.semaphore_wait(barrier, 1 + below + below_z + place(x))
    signal_ring(ring_reply, False)

    few, most, every = pl.ds(0, FIRST), pl.ds(FIRST, COLS - FIRST), pl.ds(0, COLS)
    pieces = [
        (d, start, rows, cols)
        for start, rows, cols in (
            (0, CHUNK, few), (0, CHUNK, most), (CHUNK, HALF - CHUNK, every)
        )
        for d in (0, 1)
    ]
    tails = [pl.ds(FULL, CORNER), pl.ds(0, FULL)]
    own_way = {
        3: [(0, CHUNK, pl.ds(FIRST, FULL - FIRST))],
        4: [(CHUNK, HALF - 2 * CHUNK, every), (HALF - CHUNK, CHUNK, tails[1])],
    }
    for i, (d, start, rows, cols) in enumerate(pieces):
        if i == 4:
            wait(load_sem.at[3], g.at[pl.ds(at(2, 0), 2 * OWN - 2 * CHUNK)])
            for e in (0, 1):
                widen(2, e * HALF + CHUNK, HALF - CHUNK)
        to_partner(2, d * HALF + start, rows, i, cols)
    for i, (d, start, rows, cols) in enumerate(pieces):
        here = (2, pl.ds(d * HALF + start, rows), cols)
        wait(p_rs.at[i], precv.at[here])
        add_own(2, d * HALF + start, rows, cols)
        if i == 0:

            @pl.when(below < 2)
            def _():
                pl.semaphore_wait(ring_reply, 2 - below)

        for start, rows, cols in own_way.get(i, [(start, rows, cols)]):
            send(
                precv.at[2, pl.ds(d * HALF + start, rows), cols],
                far.at[d, pl.ds(start, rows), cols], far_sent, f_rs.at[0], (up, down)[d],
            )
    for r, odd in ((0, 3), (1, 1)):
        source = precv.at[2, pl.ds(CORNER_ROWS[r], CHUNK), tails[0]]
        for way in (0, 1):

            @pl.when((y == odd) == (way != r))
            def _(r=r, way=way, source=source):
                send(source, corner.at[way, r], corner_sent, f_rs.at[1], (up, down)[way])

    signal_far(reply, False)
    for peer in (up, down):
        signal(ring, peer)

    q_load.wait()
    qs[pl.ds(0, 3 * RANK), :] = split3(q[...])
    qs[pl.ds(3 * RANK, RANK), :] = jnp.zeros((RANK, COLS), BF16)
    e_load.wait()

    def split_error(i, carry):
        at_row = pl.multiple_of(i * CHUNK, CHUNK)
        for j, term in enumerate(split(err[pl.ds(at_row, CHUNK), :])):
            g[pl.ds(ROWS + j * OWN + at_row, CHUNK), :] = term
        return carry

    lax.fori_loop(0, OWN // CHUNK, split_error, 0)
    wait(load_sem.at[4], g.at[pl.ds(0, 3 * 2 * OWN)])
    answers = (NZ - 1 - z) - ((z == 3) | (z == 4)) + (NX - 1 - place(x))

    @pl.when(z == NZ - 2)
    def _():
        pl.semaphore_wait(reply, answers)
        for j in (1, NZ - 2, NZ - 3):
            signal(known, z_peers[j - 1])

    def send_near(d, start, rows, i, cols=slice(None)):
        window = (pl.ds(start, rows), cols)
        send(
            precv.at[((1, 3)[d], *window)],
            near.at[(d, *window)],
            near_sent, n_rs.at[i], (up, down)[d],
        )

    def widen_early():
        widen(1, HALF, HALF)
        to_partner(1, HALF, HALF, 6)
        widen(3, 0, HALF)
        to_partner(3, 0, HALF, 6)

    def near_early():
        wait(p_rs.at[6], precv.at[0])
        add_own(1, HALF, HALF)
        send_near(0, HALF + CHUNK, HALF - CHUNK, 0)
        send_near(0, HALF, CHUNK, 0, tails[1])
        add_own(3, 0, HALF)
        send_near(1, 0, HALF - CHUNK, 0)
        send_near(1, HALF - CHUNK, CHUNK, 0, tails[1])

    def widen_rest():
        widen(1, 0, HALF)
        to_partner(1, 0, HALF, 7)
        widen(3, HALF, HALF)
        to_partner(3, HALF, HALF, 7)
        widen(0, 0, OWN)
        to_partner(0, 0, OWN, 7)

    def near_late():
        wait(p_rs.at[7], precv.at[pl.ds(0, 2)])
        wait(f_rs.at[0], but_corners)

        @pl.when(y % 2 == 1)
        def _():
            wait(f_rs.at[1], corner.at[0])

        @pl.when(y == 2)
        def _():
            wait(f_rs.at[1], corner)

        for d, k in ((0, 1), (1, 3)):
            for r in (0, 1):
                here = (k, pl.ds(CORNER_ROWS[r], CHUNK), tails[0])
                precv[here] += corner[d, r]
            send_near(d, CORNER_ROWS[1 - d], CHUNK, 3, tails[0])
        for d, k, half in ((0, 1, 0), (1, 3, HALF)):

            def step(j, carry, d=d, k=k, half=half):
                at_row = pl.multiple_of(j * CHUNK, CHUNK)
                here = pl.ds(half + at_row, CHUNK)
                precv[k, here, :] = (
                    precv[k, here, :]
                    + g[pl.ds(at(k, 0) + half + at_row, CHUNK), :].astype(F32)
                    + far[d, pl.ds(at_row, CHUNK), :]
                )
                return carry

            lax.fori_loop(0, HALF // CHUNK, step, 0)
        for i, (first, rows) in enumerate(LAST):
            for d, half in ((0, 0), (1, HALF)):
                send_near(d, half + first, rows, 1 + i)

    def add_near(d, start, rows):
        def step(j, carry):
            here = pl.ds(pl.multiple_of(start + j * 8, 8), 8)
            new_error[here, :] += near[d, here, :]
            return carry

        lax.fori_loop(0, rows // 8, step, 0)

    def merge_own():
        def step(i, carry):
            here = pl.ds(pl.multiple_of(i * CHUNK, CHUNK), CHUNK)
            new_error[here, :] = (
                precv[0, here, :] + g[here, :].astype(F32) + err[here, :]
            )
            return carry

        lax.fori_loop(0, OWN // CHUNK, step, 0)

    def merge_early():
        wait(n_rs.at[0], but_corners)
        wait(n_rs.at[3], corner.at[0])
        add_near(0, HALF, HALF)
        add_near(1, 0, HALF)

    def all_reduce(width, bufs, sems, beside):
        part, core_in, z_in, x_all, x_sum, y_all, full = bufs
        piece = width // NZ
        mine = pl.multiple_of(16 * c, 16)
        theirs = pl.multiple_of(16 * (1 - c), 16)
        at_z = pl.multiple_of(piece * z, 128)

        def phase(name, i, copies, like):
            for src, dst, peer in copies:
                send(src, dst, sum_sent, sems.at[i], peer)
            beside(name)
            wait(sems.at[i], like)
            wait(sum_sent, like)

        phase("core", 0, [(part.at[pl.ds(theirs, 16)], core_in, partner)], core_in)
        core_in[...] += part[pl.ds(mine, 16), :]

        def there(j):
            return pl.ds(pl.multiple_of(piece * ((z + j + 1) % NZ), 128), piece)

        phase(
            "z", 1, [(core_in.at[:, there(j)], z_in.at[j], peer) for j, peer in enumerate(z_peers)], z_in
        )
        total = core_in[:, pl.ds(at_z, piece)]
        for j in range(NZ - 1):
            total = total + z_in[j]
        x_all[x] = total
        phase(
            "x", 2, [(x_all.at[x], x_all.at[x], peer) for peer in x_peers], x_all.at[pl.ds(0, NX - 1)]
        )
        total = (x_all[0] + x_all[1]) + (x_all[2] + x_all[3])
        quartered = y_all.shape[-1] < piece
        if quartered:
            quarter = piece // NX
            x_sum[...] = total
            y_all[y] = x_sum[:, pl.ds(pl.multiple_of(quarter * x, 128), quarter)]
            source = x_sum.at[:, pl.ds(pl.multiple_of(quarter * ((x + 1) % NX), 128), quarter)]
            window = (pl.ds(mine, 16), pl.ds(pl.multiple_of(at_z + quarter * x, 128), quarter))
        else:
            y_all[y] = total
            source = y_all.at[y]
            window = (pl.ds(mine, 16), pl.ds(at_z, piece))
        three = y_all.at[pl.ds(0, NY - 1)]
        phase("y", 3, [(source, y_all.at[y], peer) for peer in y_peers], three)
        full[window] = (y_all[0] + y_all[1]) + (y_all[2] + y_all[3])
        if quartered:
            phase("x2", 4, [(full.at[window], full.at[window], peer) for peer in x_peers], three)
            window = (pl.ds(mine, 16), pl.ds(at_z, piece))
        phase("z2", 5, [(full.at[window], full.at[window], peer) for peer in z_peers], z_in)
        window = (pl.ds(mine, 16),)
        phase("core2", 6, [(full.at[window], full.at[window], partner)], core_in)

    part_f = bufs_f[0]

    def left_terms(start, rows):
        terms = lax.dot_general(
            g[pl.ds(start, rows), :], qs[...], NT, preferred_element_type=F32
        )
        return fold3(terms.T)

    for k in (1, 2, 3):
        terms = left_terms(at(k, 0), 2 * OWN)
        for t in (0, 1):
            part_f[:, pl.ds(first_row(k, t), OWN)] = terms[:, OWN * t : OWN * (t + 1)]
    terms = left_terms(0, 2 * OWN)
    own = left_terms(ROWS, 3 * OWN)
    part_f[:, pl.ds(first_row(0, 1), OWN)] = terms[:, OWN:]
    part_f[:, pl.ds(first_row(0, 0), OWN)] = (
        terms[:, :OWN] + own[:, :OWN] + own[:, OWN : 2 * OWN] + own[:, 2 * OWN :]
    )

    def beside_f(phase):
        if phase == "core":
            pl.semaphore_wait(ring, 2)
            @pl.when((answers > 0) & (z != NZ - 2))
            def _():
                pl.semaphore_wait(reply, answers)

            @pl.when((z == 3) | (z == 4) | (z == NZ - 1))
            def _():
                pl.semaphore_wait(known, 1)

        elif phase == "z":
            widen_early()
        elif phase == "x":
            near_early()
        elif phase == "y":
            widen_rest()
        elif phase == "z2":
            near_late()

    all_reduce(ROWS, bufs_f, ar_f, beside_f)
    factor = bufs_f[6]

    for k in range(NY):
        for t in (0, 1):
            fs[:, pl.ds(at(k, t), OWN)] = split3(factor[:, pl.ds(first_row(k, t), OWN)])
    own_factor = factor[:, pl.ds(first_row(0, 0), OWN)]
    for j in range(3):
        fs[:, pl.ds(ROWS + j * OWN, OWN)] = split3(own_factor)
    part_u = bufs_u[0]
    for start in range(0, COLS, 1024):
        cols = pl.ds(start, min(1024, COLS - start))
        part_u[:, cols] = fold3(
            lax.dot_general(fs[...], g[:, cols], NN, preferred_element_type=F32)
        )
    part_u[:, pl.ds(COLS, WIDE - COLS)] = jnp.zeros((RANK, WIDE - COLS), F32)

    def beside_u(phase):
        if phase == "z":
            merge_own()
            whole = factor[...]
            gram = lax.dot_general(whole, whole, NT, precision=HIGHEST, preferred_element_type=F32)
            linv = inverse_lower(gram)
            linv6[...] = left6((linv * (1.0 / (NX * NZ))).T)
            basis = lax.dot_general(
                linv, own_factor, NN, precision=HIGHEST, preferred_element_type=F32
            )
            basis6[...] = left6(basis)
        elif phase == "z2":
            merge_early()

    all_reduce(WIDE, bufs_u, ar_u, beside_u)
    for start in range(0, COLS, 1024):
        cols = pl.ds(start, min(1024, COLS - start))
        right = lax.dot_general(
            linv6[...], right6(bufs_u[6][:, cols]), NN, preferred_element_type=F32
        )
        q_next[:, cols] = right
        value = lax.dot_general(basis6[...], right6(right), NN, preferred_element_type=F32)
        approx[:, cols] = value
        new_error[:, cols] -= value
    wait(to_partner_sent, psend)
    wait(far_sent, but_corners)
    wait(corner_sent, corner.at[0])
    for i, (first, rows) in enumerate(LAST):
        wait(n_rs.at[1 + i], near.at[0, pl.ds(0, 2 * rows)])
        add_near(0, first, rows)
        add_near(1, HALF + first, rows)
    wait(near_sent, near)


def reduce_buffers(width, quartered):
    piece = width // NZ
    return (
        pltpu.VMEM((RANK, width), F32),
        pltpu.VMEM((16, width), F32),
        pltpu.VMEM((NZ - 1, 16, piece), F32),
        pltpu.VMEM((NX, 16, piece), F32),
        pltpu.VMEM((16, piece), F32),
        pltpu.VMEM((NY, 16, piece // NX if quartered else piece), F32),
        pltpu.VMEM((RANK, width), F32),
    )


def out_kernel(approx, new_error, q_next, approx_out, new_error_out, q_out, sem):
    copies = [
        pltpu.make_async_copy(approx, approx_out, sem.at[0]),
        pltpu.make_async_copy(new_error, new_error_out.at[0], sem.at[1]),
        pltpu.make_async_copy(q_next, q_out, sem.at[2]),
    ]
    for copy in copies:
        copy.start()
    for copy in copies:
        copy.wait()


def body(grads, error, q_factor):
    any_space = pl.BlockSpec(memory_space=pl.ANY)
    vmem = pl.BlockSpec(memory_space=pltpu.VMEM)
    dma = pltpu.SemaphoreType.DMA
    results = pl.pallas_call(
        main_kernel,
        out_shape=(
            pltpu.VMEM((OWN, COLS), F32),
            pltpu.VMEM((OWN, COLS), F32),
            pltpu.VMEM((RANK, COLS), F32),
        ),
        in_specs=[any_space] * 3,
        out_specs=(vmem,) * 3,
        scratch_shapes=[
            pltpu.VMEM((ROWS + 3 * OWN, COLS), BF16),
            pltpu.VMEM((OWN, COLS), F32),
            pltpu.VMEM((RANK, COLS), F32),
            pltpu.VMEM((4 * RANK, COLS), BF16),
            pltpu.VMEM((NY, OWN, COLS), F32),
            pltpu.VMEM((NY, OWN, COLS), F32),
            pltpu.VMEM((2, HALF, COLS), F32),
            pltpu.VMEM((2, 2, CHUNK, CORNER), F32),
            pltpu.VMEM((2, OWN, COLS), F32),
            pltpu.VMEM((3 * RANK, ROWS + 3 * OWN), BF16),
            pltpu.VMEM((RANK, 6 * RANK), BF16),
            pltpu.VMEM((OWN, 6 * RANK), BF16),
            reduce_buffers(ROWS, False),
            reduce_buffers(WIDE, True),
            dma((5,)),
            dma((5,)),
            dma((8,)),
            dma((2,)),
            dma((4,)),
            dma((7,)),
            dma((7,)),
            pltpu.SemaphoreType.REGULAR,
            pltpu.SemaphoreType.REGULAR,
            pltpu.SemaphoreType.REGULAR,
            pltpu.SemaphoreType.REGULAR,
        ],
        compiler_params=pltpu.CompilerParams(
            collective_id=0, has_side_effects=True, vmem_limit_bytes=48 << 20
        ),
        cost_estimate=pl.CostEstimate(
            flops=1 << 31, bytes_accessed=14 << 20, transcendentals=0
        ),
    )(grads, error, pltpu.with_memory_space_constraint(q_factor, pltpu.HBM))
    return pl.pallas_call(
        out_kernel,
        out_shape=(
            jax.ShapeDtypeStruct((OWN, COLS), F32),
            jax.ShapeDtypeStruct((1, OWN, COLS), F32),
            jax.ShapeDtypeStruct((RANK, COLS), F32),
        ),
        in_specs=[vmem] * 3,
        out_specs=(any_space,) * 3,
        scratch_shapes=[dma((3,))],
        compiler_params=pltpu.CompilerParams(vmem_limit_bytes=16 << 20),
    )(*results)


def solution(mesh):
    in_specs = (P("rep", "shard", None, None), P("rep", "shard", None), P())
    out_specs = (P("shard", None), P("rep", "shard", None), P())
    return jax.shard_map(body, mesh=mesh, in_specs=in_specs, out_specs=out_specs, check_vma=False)
```

```python
import functools

import jax
import jax.numpy as jnp
from jax import lax
from jax.experimental import pallas as pl
from jax.experimental.pallas import tpu as pltpu
from jax.sharding import PartitionSpec as P

MESH = pl.DeviceIdType.MESH
F32 = jnp.float32
BF16 = jnp.bfloat16
HIGHEST = lax.Precision.HIGHEST
ROWS, COLS, RANK = 1024, 3968, 32
NX, NY, NZ = 4, 4, 8
OWN = 128
HALF = OWN // 2
CHUNK = 16
FIRST = 1024
LAST = ((0, HALF - 8), (HALF - 8, 8))
CORNER = 768
FULL = COLS - CORNER
CORNER_ROWS = (HALF - CHUNK, HALF)
WIDE = 4096
NT = (((1,), (1,)), ((), ()))
NN = (((1,), (0,)), ((), ()))


def split(value):
    high = value.astype(BF16)
    rest = value - high.astype(F32)
    middle = rest.astype(BF16)
    low = (rest - middle.astype(F32)).astype(BF16)
    return high, middle, low


def split3(value):
    return jnp.concatenate(split(value), axis=0)


def left6(value):
    high, middle, low = (term.astype(F32) for term in split(value))
    return jnp.concatenate([high, high, middle, high, low, middle], axis=0).T.astype(BF16)


def right6(value):
    high, middle, low = split(value)
    return jnp.concatenate([high, middle, high, low, high, middle], axis=0)


def fold3(value):
    return value[:RANK] + value[RANK : 2 * RANK] + value[2 * RANK : 3 * RANK]


def inverse_lower(gram):
    row = lax.broadcasted_iota(jnp.int32, (RANK, 2 * RANK), 0)
    col = lax.broadcasted_iota(jnp.int32, (RANK, 2 * RANK), 1)
    work = jnp.concatenate([gram, jnp.zeros((RANK, RANK), F32)], axis=1)
    work = jnp.where(col == row + RANK, 1.0, work)
    scale = jnp.zeros((RANK, 1), F32)
    row1 = lax.broadcasted_iota(jnp.int32, (RANK, 1), 0)
    for j in range(RANK):
        pivot_row = work[j : j + 1, :]
        pivot = work[j : j + 1, j : j + 1]
        factor = jnp.where(row1 > j, work[:, j : j + 1] / pivot, 0.0)
        scale = jnp.where(row1 == j, 1.0 / jnp.sqrt(pivot), scale)
        work = work - factor * pivot_row
    return work[:, RANK:] * scale


def main_kernel(
    g_hbm, e_hbm, q_hbm,
    approx, new_error, q_next,
    g, err, q, qs, psend, precv, far, corner, near, fs, linv6, basis6,
    bufs_f, bufs_u,
    load_sem, sent_sem, p_rs, f_rs, n_rs, ar_f, ar_u, reply, known, ring_reply, ring,
):
    rep, shard = lax.axis_index("rep"), lax.axis_index("shard")
    x, z = rep // NZ, rep % NZ
    y, c = shard // 2, shard % 2

    def dev(dx, dy, dz, dc):
        return (
            ((x + dx) % NX) * NZ + (z + dz) % NZ,
            ((y + dy) % NY) * 2 + (c + dc) % 2,
        )

    partner = dev(0, 0, 0, 1)
    up, down = dev(0, 1, 0, 0), dev(0, NY - 1, 0, 0)
    x_peers = [dev(j, 0, 0, 0) for j in range(1, NX)]
    z_peers = [dev(0, 0, j, 0) for j in range(1, NZ)]
    y_peers = [dev(1, j, 0, 0) for j in range(1, NY)]
    barrier = pltpu.get_barrier_semaphore()

    def signal(semaphore, peer):
        pl.semaphore_signal(semaphore, 1, device_id=peer, device_id_type=MESH)

    def place(at):
        return at + (at == 2) - (at == 3)

    def signal_ring(semaphore, above):
        for j, peer in ((1, up), (3, down)):
            pl.when((place((y + j) % NY) > place(y)) == above)(
                functools.partial(signal, semaphore, peer)
            )

    def signal_far(semaphore, above):
        for j, peer in enumerate(z_peers):
            greets = (z + j + 1 < NZ) == above
            if j == 2:
                greets = greets & (z != 4)
            elif j == 3:
                greets = greets & (z % 4 != 3)
            elif j == 4:
                greets = greets & (z != NZ - 1)
            pl.when(greets)(functools.partial(signal, semaphore, peer))
        for j, peer in enumerate(x_peers):
            pl.when((place((x + j + 1) % NX) > place(x)) == above)(functools.partial(signal, semaphore, peer))

    def send(src, dst, ss, rs, to):
        pltpu.make_async_remote_copy(
            src_ref=src, dst_ref=dst, send_sem=ss, recv_sem=rs,
            device_id=to, device_id_type=MESH,
        ).start()

    def wait(semaphore, like):
        pltpu.make_async_copy(like, like, semaphore).wait()

    but_corners = g.at[pl.ds(0, 59 * 16), pl.ds(0, 8 * 128)]

    to_partner_sent, ring_sent, sum_sent = (sent_sem.at[i] for i in range(3))

    def first_row(k, t):
        return pl.multiple_of(OWN * (2 * ((y + k) % NY) + (c + t) % 2), OWN)

    def at(k, t):
        return OWN * (2 * k + t)

    signal(barrier, partner)
    corner[...] = jnp.zeros(corner.shape, F32)
    for d in (0, 1):
        far[d, pl.ds((1 - d) * (HALF - CHUNK), CHUNK), pl.ds(FULL, CORNER)] = jnp.zeros(
            (CHUNK, CORNER), F32
        )
    signal_ring(barrier, True)
    q_load = pltpu.make_async_copy(q_hbm, q, load_sem.at[0])
    e_load = pltpu.make_async_copy(e_hbm.at[0], err, load_sem.at[1])
    def load_far(t, start, rows, i):
        for d in (0, 1):
            pltpu.make_async_copy(
                g_hbm.at[0, 0, pl.ds(first_row(2, t) + d * HALF + start, rows)],
                g.at[pl.ds(at(2, t) + d * HALF + start, rows)],
                load_sem.at[i],
            ).start()

    load_far(1, 0, CHUNK, 2)
    signal_far(barrier, True)
    load_far(0, 0, CHUNK, 3)
    load_far(1, CHUNK, HALF - CHUNK, 3)
    load_far(0, CHUNK, HALF - CHUNK, 3)

    def widen(k, start, rows):
        def step(i, carry):
            at_row = pl.multiple_of(start + i * CHUNK, CHUNK)
            psend[k, pl.ds(at_row, CHUNK), :] = g[
                pl.ds(at(k, 1) + at_row, CHUNK), :
            ].astype(F32)
            return carry

        lax.fori_loop(0, rows // CHUNK, step, 0)

    def to_partner(k, start, rows, i, cols=slice(None)):
        window = (k, pl.ds(start, rows), cols)
        send(psend.at[window], precv.at[window], to_partner_sent, p_rs.at[i], partner)

    def add_own(k, start, rows, cols=slice(None)):
        def step(i, carry):
            at_row = pl.multiple_of(start + i * CHUNK, CHUNK)
            precv[k, pl.ds(at_row, CHUNK), cols] += g[
                pl.ds(at(k, 0) + at_row, CHUNK), cols
            ].astype(F32)
            return carry

        lax.fori_loop(0, rows // CHUNK, step, 0)

    wait(load_sem.at[2], g.at[pl.ds(at(2, 1), 2 * CHUNK)])
    for d in (0, 1):
        widen(2, d * HALF, CHUNK)
    q_load.start()
    e_load.start()
    for k in (1, 3, 0):
        for t in (1, 0):
            pltpu.make_async_copy(
                g_hbm.at[0, 0, pl.ds(first_row(k, t), OWN)],
                g.at[pl.ds(at(k, t), OWN)],
                load_sem.at[4],
            ).start()
    below = jnp.minimum(y, NY - y)
    below_z = z - 2 * (z // (NZ - 1))
    pl.semaphore_wait(barrier, 1 + below + below_z + place(x))
    signal_ring(ring_reply, False)

    few, most, every = pl.ds(0, FIRST), pl.ds(FIRST, COLS - FIRST), pl.ds(0, COLS)
    pieces = [
        (d, start, rows, cols)
        for start, rows, cols in (
            (0, CHUNK, few), (0, CHUNK, most), (CHUNK, HALF - CHUNK, every)
        )
        for d in (0, 1)
    ]
    tails = [pl.ds(FULL, CORNER), pl.ds(0, FULL)]
    own_way = {
        3: [(0, CHUNK, pl.ds(FIRST, FULL - FIRST))],
        4: [(CHUNK, HALF - 2 * CHUNK, every), (HALF - CHUNK, CHUNK, tails[1])],
    }
    for i, (d, start, rows, cols) in enumerate(pieces):
        if i == 4:
            wait(load_sem.at[3], g.at[pl.ds(at(2, 0), 2 * OWN - 2 * CHUNK)])
            for e in (0, 1):
                widen(2, e * HALF + CHUNK, HALF - CHUNK)
        to_partner(2, d * HALF + start, rows, i, cols)
    for i, (d, start, rows, cols) in enumerate(pieces):
        here = (2, pl.ds(d * HALF + start, rows), cols)
        wait(p_rs.at[i], precv.at[here])
        add_own(2, d * HALF + start, rows, cols)
        if i == 0:

            @pl.when(below < 2)
            def _():
                pl.semaphore_wait(ring_reply, 2 - below)

        for start, rows, cols in own_way.get(i, [(start, rows, cols)]):
            send(
                precv.at[2, pl.ds(d * HALF + start, rows), cols],
                far.at[d, pl.ds(start, rows), cols], ring_sent, f_rs.at[0], (up, down)[d],
            )
    for r, odd in ((0, 3), (1, 1)):
        source = precv.at[2, pl.ds(CORNER_ROWS[r], CHUNK), tails[0]]
        for way in (0, 1):

            @pl.when((y == odd) == (way != r))
            def _(r=r, way=way, source=source):
                send(source, corner.at[way, r], ring_sent, f_rs.at[1], (up, down)[way])

    signal_far(reply, False)
    for peer in (up, down):
        signal(ring, peer)

    q_load.wait()
    qs[pl.ds(0, 3 * RANK), :] = split3(q[...])
    qs[pl.ds(3 * RANK, RANK), :] = jnp.zeros((RANK, COLS), BF16)
    e_load.wait()

    def split_error(i, carry):
        at_row = pl.multiple_of(i * CHUNK, CHUNK)
        for j, term in enumerate(split(err[pl.ds(at_row, CHUNK), :])):
            g[pl.ds(ROWS + j * OWN + at_row, CHUNK), :] = term
        return carry

    lax.fori_loop(0, OWN // CHUNK, split_error, 0)
    wait(load_sem.at[4], g.at[pl.ds(0, 3 * 2 * OWN)])
    answers = (NZ - 1 - z) - ((z == 3) | (z == 4)) + (NX - 1 - place(x))

    @pl.when(z == NZ - 2)
    def _():
        pl.semaphore_wait(reply, answers)
        for j in (1, NZ - 2, NZ - 3):
            signal(known, z_peers[j - 1])

    def send_near(d, start, rows, i, cols=slice(None)):
        window = (pl.ds(start, rows), cols)
        send(
            precv.at[((1, 3)[d], *window)],
            near.at[(d, *window)],
            ring_sent, n_rs.at[i], (up, down)[d],
        )

    def widen_early():
        widen(1, HALF, HALF)
        to_partner(1, HALF, HALF, 6)
        widen(3, 0, HALF)
        to_partner(3, 0, HALF, 6)

    def near_early():
        wait(p_rs.at[6], precv.at[0])
        add_own(1, HALF, HALF)
        send_near(0, HALF + CHUNK, HALF - CHUNK, 0)
        send_near(0, HALF, CHUNK, 0, tails[1])
        add_own(3, 0, HALF)
        send_near(1, 0, HALF - CHUNK, 0)
        send_near(1, HALF - CHUNK, CHUNK, 0, tails[1])

    def widen_rest():
        widen(1, 0, HALF)
        to_partner(1, 0, HALF, 7)
        widen(3, HALF, HALF)
        to_partner(3, HALF, HALF, 7)
        widen(0, 0, OWN)
        to_partner(0, 0, OWN, 7)

    def near_late():
        wait(p_rs.at[7], precv.at[pl.ds(0, 2)])
        wait(f_rs.at[0], but_corners)

        @pl.when(y % 2 == 1)
        def _():
            wait(f_rs.at[1], corner.at[0])

        @pl.when(y == 2)
        def _():
            wait(f_rs.at[1], corner)

        for d, k in ((0, 1), (1, 3)):
            for r in (0, 1):
                here = (k, pl.ds(CORNER_ROWS[r], CHUNK), tails[0])
                precv[here] += corner[d, r]
            send_near(d, CORNER_ROWS[1 - d], CHUNK, 3, tails[0])
        for d, k, half in ((0, 1, 0), (1, 3, HALF)):

            def step(j, carry, d=d, k=k, half=half):
                at_row = pl.multiple_of(j * CHUNK, CHUNK)
                here = pl.ds(half + at_row, CHUNK)
                precv[k, here, :] = (
                    precv[k, here, :]
                    + g[pl.ds(at(k, 0) + half + at_row, CHUNK), :].astype(F32)
                    + far[d, pl.ds(at_row, CHUNK), :]
                )
                return carry

            lax.fori_loop(0, HALF // CHUNK, step, 0)
        for i, (first, rows) in enumerate(LAST):
            for d, half in ((0, 0), (1, HALF)):
                send_near(d, half + first, rows, 1 + i)

    def add_near(d, start, rows):
        def step(j, carry):
            here = pl.ds(pl.multiple_of(start + j * 8, 8), 8)
            new_error[here, :] += near[d, here, :]
            return carry

        lax.fori_loop(0, rows // 8, step, 0)

    def merge_own():
        def step(i, carry):
            here = pl.ds(pl.multiple_of(i * CHUNK, CHUNK), CHUNK)
            new_error[here, :] = (
                precv[0, here, :] + g[here, :].astype(F32) + err[here, :]
            )
            return carry

        lax.fori_loop(0, OWN // CHUNK, step, 0)

    def merge_early():
        wait(n_rs.at[0], but_corners)
        wait(n_rs.at[3], corner.at[0])
        add_near(0, HALF, HALF)
        add_near(1, 0, HALF)

    def all_reduce(width, bufs, sems, beside):
        part, core_in, z_in, x_all, x_sum, y_all, full = bufs
        piece = width // NZ
        mine = pl.multiple_of(16 * c, 16)
        theirs = pl.multiple_of(16 * (1 - c), 16)
        at_z = pl.multiple_of(piece * z, 128)

        def phase(name, i, copies, like):
            for src, dst, peer in copies:
                send(src, dst, sum_sent, sems.at[i], peer)
            beside(name)
            wait(sems.at[i], like)
            wait(sum_sent, like)

        phase("core", 0, [(part.at[pl.ds(theirs, 16)], core_in, partner)], core_in)
        core_in[...] += part[pl.ds(mine, 16), :]

        def there(j):
            return pl.ds(pl.multiple_of(piece * ((z + j + 1) % NZ), 128), piece)

        phase(
            "z", 1, [(core_in.at[:, there(j)], z_in.at[j], peer) for j, peer in enumerate(z_peers)], z_in
        )
        total = core_in[:, pl.ds(at_z, piece)]
        for j in range(NZ - 1):
            total = total + z_in[j]
        x_all[x] = total
        phase(
            "x", 2, [(x_all.at[x], x_all.at[x], peer) for peer in x_peers], x_all.at[pl.ds(0, NX - 1)]
        )
        total = (x_all[0] + x_all[1]) + (x_all[2] + x_all[3])
        quartered = y_all.shape[-1] < piece
        if quartered:
            quarter = piece // NX
            x_sum[...] = total
            y_all[y] = x_sum[:, pl.ds(pl.multiple_of(quarter * x, 128), quarter)]
            source = x_sum.at[:, pl.ds(pl.multiple_of(quarter * ((x + 1) % NX), 128), quarter)]
            window = (pl.ds(mine, 16), pl.ds(pl.multiple_of(at_z + quarter * x, 128), quarter))
        else:
            y_all[y] = total
            source = y_all.at[y]
            window = (pl.ds(mine, 16), pl.ds(at_z, piece))
        three = y_all.at[pl.ds(0, NY - 1)]
        phase("y", 3, [(source, y_all.at[y], peer) for peer in y_peers], three)
        full[window] = (y_all[0] + y_all[1]) + (y_all[2] + y_all[3])
        if quartered:
            phase("x2", 4, [(full.at[window], full.at[window], peer) for peer in x_peers], three)
            window = (pl.ds(mine, 16), pl.ds(at_z, piece))
        phase("z2", 5, [(full.at[window], full.at[window], peer) for peer in z_peers], z_in)
        window = (pl.ds(mine, 16),)
        phase("core2", 6, [(full.at[window], full.at[window], partner)], core_in)

    part_f = bufs_f[0]

    def left_terms(start, rows):
        terms = lax.dot_general(
            g[pl.ds(start, rows), :], qs[...], NT, preferred_element_type=F32
        )
        return fold3(terms.T)

    for k in (1, 2, 3):
        terms = left_terms(at(k, 0), 2 * OWN)
        for t in (0, 1):
            part_f[:, pl.ds(first_row(k, t), OWN)] = terms[:, OWN * t : OWN * (t + 1)]
    terms = left_terms(0, 2 * OWN)
    own = left_terms(ROWS, 3 * OWN)
    part_f[:, pl.ds(first_row(0, 1), OWN)] = terms[:, OWN:]
    part_f[:, pl.ds(first_row(0, 0), OWN)] = (
        terms[:, :OWN] + own[:, :OWN] + own[:, OWN : 2 * OWN] + own[:, 2 * OWN :]
    )

    def beside_f(phase):
        if phase == "core":
            pl.semaphore_wait(ring, 2)
            @pl.when((answers > 0) & (z != NZ - 2))
            def _():
                pl.semaphore_wait(reply, answers)

            @pl.when((z == 3) | (z == 4) | (z == NZ - 1))
            def _():
                pl.semaphore_wait(known, 1)

        elif phase == "z":
            widen_early()
        elif phase == "x":
            near_early()
        elif phase == "y":
            widen_rest()
        elif phase == "z2":
            near_late()

    all_reduce(ROWS, bufs_f, ar_f, beside_f)
    factor = bufs_f[6]

    for k in range(NY):
        for t in (0, 1):
            fs[:, pl.ds(at(k, t), OWN)] = split3(factor[:, pl.ds(first_row(k, t), OWN)])
    own_factor = factor[:, pl.ds(first_row(0, 0), OWN)]
    for j in range(3):
        fs[:, pl.ds(ROWS + j * OWN, OWN)] = split3(own_factor)
    part_u = bufs_u[0]
    for start in range(0, COLS, 1024):
        cols = pl.ds(start, min(1024, COLS - start))
        part_u[:, cols] = fold3(
            lax.dot_general(fs[...], g[:, cols], NN, preferred_element_type=F32)
        )
    part_u[:, pl.ds(COLS, WIDE - COLS)] = jnp.zeros((RANK, WIDE - COLS), F32)

    def beside_u(phase):
        if phase == "z":
            merge_own()
            whole = factor[...]
            gram = lax.dot_general(whole, whole, NT, precision=HIGHEST, preferred_element_type=F32)
            linv = inverse_lower(gram)
            linv6[...] = left6((linv * (1.0 / (NX * NZ))).T)
            basis = lax.dot_general(
                linv, own_factor, NN, precision=HIGHEST, preferred_element_type=F32
            )
            basis6[...] = left6(basis)
        elif phase == "z2":
            merge_early()

    all_reduce(WIDE, bufs_u, ar_u, beside_u)
    for start in range(0, COLS, 1024):
        cols = pl.ds(start, min(1024, COLS - start))
        right = lax.dot_general(
            linv6[...], right6(bufs_u[6][:, cols]), NN, preferred_element_type=F32
        )
        q_next[:, cols] = right
        value = lax.dot_general(basis6[...], right6(right), NN, preferred_element_type=F32)
        approx[:, cols] = value
        new_error[:, cols] -= value
    wait(to_partner_sent, psend)
    for i, (first, rows) in enumerate(LAST):
        wait(n_rs.at[1 + i], near.at[0, pl.ds(0, 2 * rows)])
        add_near(0, first, rows)
        add_near(1, HALF + first, rows)
    wait(ring_sent, psend.at[pl.ds(0, 3)])


def reduce_buffers(width, quartered):
    piece = width // NZ
    return (
        pltpu.VMEM((RANK, width), F32),
        pltpu.VMEM((16, width), F32),
        pltpu.VMEM((NZ - 1, 16, piece), F32),
        pltpu.VMEM((NX, 16, piece), F32),
        pltpu.VMEM((16, piece), F32),
        pltpu.VMEM((NY, 16, piece // NX if quartered else piece), F32),
        pltpu.VMEM((RANK, width), F32),
    )


def out_kernel(approx, new_error, q_next, approx_out, new_error_out, q_out, sem):
    copies = [
        pltpu.make_async_copy(approx, approx_out, sem.at[0]),
        pltpu.make_async_copy(new_error, new_error_out.at[0], sem.at[1]),
        pltpu.make_async_copy(q_next, q_out, sem.at[2]),
    ]
    for copy in copies:
        copy.start()
    for copy in copies:
        copy.wait()


def body(grads, error, q_factor):
    any_space = pl.BlockSpec(memory_space=pl.ANY)
    vmem = pl.BlockSpec(memory_space=pltpu.VMEM)
    dma = pltpu.SemaphoreType.DMA
    results = pl.pallas_call(
        main_kernel,
        out_shape=(
            pltpu.VMEM((OWN, COLS), F32),
            pltpu.VMEM((OWN, COLS), F32),
            pltpu.VMEM((RANK, COLS), F32),
        ),
        in_specs=[any_space] * 3,
        out_specs=(vmem,) * 3,
        scratch_shapes=[
            pltpu.VMEM((ROWS + 3 * OWN, COLS), BF16),
            pltpu.VMEM((OWN, COLS), F32),
            pltpu.VMEM((RANK, COLS), F32),
            pltpu.VMEM((4 * RANK, COLS), BF16),
            pltpu.VMEM((NY, OWN, COLS), F32),
            pltpu.VMEM((NY, OWN, COLS), F32),
            pltpu.VMEM((2, HALF, COLS), F32),
            pltpu.VMEM((2, 2, CHUNK, CORNER), F32),
            pltpu.VMEM((2, OWN, COLS), F32),
            pltpu.VMEM((3 * RANK, ROWS + 3 * OWN), BF16),
            pltpu.VMEM((RANK, 6 * RANK), BF16),
            pltpu.VMEM((OWN, 6 * RANK), BF16),
            reduce_buffers(ROWS, False),
            reduce_buffers(WIDE, True),
            dma((5,)),
            dma((3,)),
            dma((8,)),
            dma((2,)),
            dma((4,)),
            dma((7,)),
            dma((7,)),
            pltpu.SemaphoreType.REGULAR,
            pltpu.SemaphoreType.REGULAR,
            pltpu.SemaphoreType.REGULAR,
            pltpu.SemaphoreType.REGULAR,
        ],
        compiler_params=pltpu.CompilerParams(
            collective_id=0, has_side_effects=True, vmem_limit_bytes=48 << 20
        ),
        cost_estimate=pl.CostEstimate(
            flops=1 << 31, bytes_accessed=14 << 20, transcendentals=0
        ),
    )(grads, error, pltpu.with_memory_space_constraint(q_factor, pltpu.HBM))
    return pl.pallas_call(
        out_kernel,
        out_shape=(
            jax.ShapeDtypeStruct((OWN, COLS), F32),
            jax.ShapeDtypeStruct((1, OWN, COLS), F32),
            jax.ShapeDtypeStruct((RANK, COLS), F32),
        ),
        in_specs=[vmem] * 3,
        out_specs=(any_space,) * 3,
        scratch_shapes=[dma((3,))],
        compiler_params=pltpu.CompilerParams(vmem_limit_bytes=16 << 20),
    )(*results)


def solution(mesh):
    in_specs = (P("rep", "shard", None, None), P("rep", "shard", None), P())
    out_specs = (P("shard", None), P("rep", "shard", None), P())
    return jax.shard_map(body, mesh=mesh, in_specs=in_specs, out_specs=out_specs, check_vma=False)
```
